128 devices in a mesh: row: 16 (over y, x), col: 8 (over z, core).
Axes of the slice: x: 4, y: 4, z: 4, core: 2. Of those that a mesh axis runs over, the one named last changes fastest.
Arguments:
- features: bfloat16 [262144, 128], P(('row', 'col')), may hold values from -6 to 6
- cotangent: bfloat16 [262144, 128], P(('row', 'col')), may hold values from -6 to 6
- self_weight: bfloat16 [128, 128], replicated, may hold values from -0.5 to 0.5
- neigh_weight: bfloat16 [128, 128], replicated, may hold values from -0.5 to 0.5
- kernel: float32 [16, 128], replicated, may hold values from 0.3 to 3
- needed: int32 [16, 8, 16, 1024], P('row', 'col'), may hold values from 0 to 2047, as said below
- src_slot: int32 [16, 8, 4096], P('row', 'col'), may hold values from 0 to 16383, as said below
- dst_local: int32 [16, 8, 4096], P('row', 'col'), may hold values from 0 to 16384, as said below
- bucket: int32 [16, 8, 4096], P('row', 'col'), may hold values from 0 to 15, as said below
Outputs:
- out_rows: bfloat16 [262144, 128], P(('row', 'col'))
- feature_grad: float32 [262144, 128], P(('row', 'col'))
- self_grad: float32 [128, 128], replicated
- neigh_grad: float32 [128, 128], replicated
- kernel_grad: float32 [16, 128], replicated
The draws below stay inside these ranges and needn't reach their ends.
Inputs may be any that keep to these rules, and one draw needn't show every extreme that they name: Each list needed[r, c, o, :] holds 1024 different local rows of owner (o, c). `src_slot`: slot value s reads entry s mod 1024 of the list for owner s // 1024. `dst_local`: the value 8 * 2048 marks a padding slot; on each device the edges come first, in whole blocks of 128, and some device has no padding. Padding slots have bucket 0.
All inputs are finite; a program needn't handle non-finite values.
Results may differ from the reference program's by a relative error of at most 0.0075.
Values may be sent and summed in bfloat16 or wider, within the bound.
No kernel may reach another device: no remote copies, remote signals or barrier semaphores. Data moves between devices by JAX's collectives and lax.ppermute only.
A program may use at most 64 MiB of HBM per device.

```python
import math
import jax
import jax.numpy as jnp
from jax import lax

F = 128
K = 16
ND = 2048
E_DEV = 4096
CAP = 1024
NODES = 262144
N_ROW = 16
N_COL = 8


def edge_fields(key):
    blocks = E_DEV // 128
    devices = N_ROW * N_COL
    keys = jax.random.split(key, 6)
    live_blocks = jax.random.randint(keys[0], (devices,), blocks // 4, blocks + 1)
    full_device = jax.random.randint(keys[1], (), 0, devices)
    live_blocks = jnp.where(jnp.arange(devices) == full_device, blocks, live_blocks)
    used = jnp.arange(E_DEV)[None, :] < live_blocks[:, None] * 128
    source = jax.random.randint(keys[2], (devices, E_DEV), 0, N_ROW * CAP)
    first = jax.random.randint(keys[3], (devices, E_DEV), 0, N_COL * ND)
    second = jax.random.randint(keys[4], (devices, E_DEV), 0, N_COL * ND)
    target = jnp.where(used, jnp.minimum(first, second), N_COL * ND)
    kinds = jnp.where(used, jax.random.randint(keys[5], (devices, E_DEV), 0, K), 0)
    shape = (N_ROW, N_COL, E_DEV)
    return (source.reshape(shape).astype(jnp.int32), target.reshape(shape).astype(jnp.int32), kinds.reshape(shape).astype(jnp.int32))


def draw_src_slot(key, part):
    return edge_fields(key)[0]


def draw_dst_local(key, part):
    return edge_fields(key)[1]


def draw_bucket(key, part):
    return edge_fields(key)[2]


def draw_needed(key, part):
    key = jax.random.fold_in(key, 7)
    scores = jax.random.randint(key, (N_ROW, N_COL, N_ROW, ND), 0, 4096) * ND + jnp.arange(ND)
    order = jnp.argsort(scores, axis=-1, stable=True)
    return order[..., :CAP].astype(jnp.int32)


def block_scale(own_key, shape, shards, smallest, largest):
    factor_of = 1.0
    for position, shards_of in shards:
        draws = jax.random.uniform(jax.random.fold_in(jax.random.fold_in(own_key, 6), position), (shards_of,), jnp.float32, smallest / len(shards), largest / len(shards))
        factor_of = factor_of * jnp.repeat(jnp.exp(draws), shape[position] // shards_of).reshape((-1,) + (1,) * (len(shape) - 1 - position))
    return factor_of


def noise(rng, shape, scale, most, cuts=(), kind=jnp.bfloat16):
    values = jax.random.normal(rng, shape, jnp.float32) * scale
    if len(cuts) > 0:
        values = block_scale(rng, shape, cuts, -0.22, 0.18) * values
    return jnp.clip(values, min=-most, max=most).astype(kind)


def setup_inputs(seed: int = 0) -> dict:
    key_of = jax.random.split(jax.random.key(seed), 10)
    features = noise(key_of[0], (NODES, F), 1.0, 6.0, ((0, 128),))
    cotangent = noise(key_of[1], (NODES, F), 1.0, 6.0, ((0, 128),))
    self_weight = noise(key_of[2], (F, F), F ** -0.5, 0.5)
    neigh_weight = noise(key_of[3], (F, F), F ** -0.5, 0.5)
    kernel = jnp.clip(jnp.exp(jax.random.uniform(key_of[4], (K, F), jnp.float32, math.log(0.3), math.log(3.0))), 0.3, 3.0)
    needed = draw_needed(jax.random.fold_in(key_of[9], 71), 0)
    src_slot = draw_src_slot(jax.random.fold_in(key_of[9], 71), 0)
    dst_local = draw_dst_local(jax.random.fold_in(key_of[9], 71), 0)
    bucket = draw_bucket(jax.random.fold_in(key_of[9], 71), 0)
    return dict(features=features, cotangent=cotangent, self_weight=self_weight, neigh_weight=neigh_weight, kernel=kernel, needed=needed, src_slot=src_slot, dst_local=dst_local, bucket=bucket)


def reference(features, cotangent, self_weight, neigh_weight, kernel, needed, src_slot, dst_local, bucket):
    nodes = N_ROW * N_COL * ND
    flat_need = needed.reshape(N_ROW, N_COL, N_ROW * CAP)
    local_src = jnp.take_along_axis(flat_need, src_slot, axis=2)
    owner = src_slot // CAP
    col_ids = jnp.arange(N_COL, dtype=jnp.int32)[None, :, None]
    row_ids = jnp.arange(N_ROW, dtype=jnp.int32)[:, None, None]
    global_src = ((owner * N_COL + col_ids) * ND + local_src).reshape(-1, E_DEV).astype(jnp.int32)
    global_dst = jnp.where(dst_local < N_COL * ND, row_ids * (N_COL * ND) + dst_local, nodes).reshape(-1, E_DEV).astype(jnp.int32)
    buckets = bucket.reshape(-1, E_DEV)

    def forward_step(carry, item):
        summed, degree = carry
        source, target, kinds = item
        messages = kernel[kinds] * features[source].astype(jnp.float32)
        return (summed.at[target].add(messages), degree.at[target].add(1.0)), None

    start = (jnp.zeros((nodes + 1, F), jnp.float32), jnp.zeros((nodes + 1,), jnp.float32))
    (summed, degree), _ = lax.scan(forward_step, start, (global_src, global_dst, buckets))
    divisor = jnp.maximum(degree[:nodes], 1.0)[:, None]
    mean = (summed[:nodes] / divisor).astype(jnp.bfloat16)
    preact = jnp.dot(features, self_weight, preferred_element_type=jnp.float32) + jnp.dot(mean, neigh_weight, preferred_element_type=jnp.float32)
    sigmoid_z = jax.nn.sigmoid(preact)
    out_rows = (preact * sigmoid_z).astype(jnp.bfloat16)
    pre_grad = (cotangent.astype(jnp.float32) * sigmoid_z * (1.0 + preact * (1.0 - sigmoid_z))).astype(jnp.bfloat16)
    rows_dims = (((0,), (0,)), ((), ()))
    self_grad = lax.dot_general(features, pre_grad, rows_dims, preferred_element_type=jnp.float32)
    neigh_grad = lax.dot_general(mean, pre_grad, rows_dims, preferred_element_type=jnp.float32)
    cols_dims = (((1,), (1,)), ((), ()))
    mean_grad = (lax.dot_general(pre_grad, neigh_weight, cols_dims, preferred_element_type=jnp.float32) / divisor).astype(jnp.bfloat16)
    padded = jnp.concatenate([mean_grad, jnp.zeros((1, F), jnp.bfloat16)], axis=0)

    def backward_step(carry, item):
        kernel_grad, neigh_dx = carry
        source, target, kinds = item
        dest_rows = padded[target].astype(jnp.float32)
        kernel_grad = kernel_grad.at[kinds].add(dest_rows * features[source].astype(jnp.float32))
        neigh_dx = neigh_dx.at[source].add(kernel[kinds] * dest_rows)
        return (kernel_grad, neigh_dx), None

    start = (jnp.zeros((K, F), jnp.float32), jnp.zeros((nodes, F), jnp.float32))
    (kernel_grad, neigh_dx), _ = lax.scan(backward_step, start, (global_src, global_dst, buckets))
    feature_grad = lax.dot_general(pre_grad, self_weight, cols_dims, preferred_element_type=jnp.float32) + neigh_dx
    return out_rows, feature_grad, self_grad, neigh_grad, kernel_grad
```

```python
import functools

import jax
import jax.numpy as jnp
from jax import lax
from jax.experimental import pallas as pl
from jax.experimental.pallas import tpu as pltpu
from jax.sharding import PartitionSpec as P

BF16 = jnp.bfloat16
F32 = jnp.float32
I32 = jnp.int32

CAP = 320
BATCH = 32
EXTRA = 64
NT = (((1,), (1,)), ((), ()))
TN = (((0,), (0,)), ((), ()))
NN = (((1,), (0,)), ((), ()))


def _dot(a, b, dims):
    return lax.dot_general(a, b, dims, preferred_element_type=F32)


def _iota(shape, dim):
    return lax.broadcasted_iota(I32, shape, dim)


def _hot(mask):
    return jnp.where(mask, 1.0, 0.0).astype(BF16)


def _plan_kernel(s_ref, d_ref, b_ref, need_ref, req_ref, dst_ref, bkt_ref, dcol_ref, num_ref, cnt_ref, p_scr):
    owners = req_ref.shape[0]
    edges = s_ref.shape[1]
    blocks = edges // 128
    rows_all = 16384
    need = need_ref[...]
    table = jnp.concatenate([(need >> 8).astype(F32), (need & 255).astype(F32)], axis=0).astype(BF16)
    s = s_ref[...]
    valid = d_ref[...] < rows_all
    owner = jnp.where(valid, s >> 10, owners)
    own = _iota((owners, edges), 0) == owner
    own_hot = _hot(own)
    stacked = jnp.concatenate([own_hot[:, b * 128 : (b + 1) * 128] for b in range(blocks)], axis=0)
    before = _hot(_iota((128, 128), 0) < _iota((128, 128), 1))
    ones = jnp.ones((128, 128), BF16)
    ranks = _dot(stacked, jnp.concatenate([before, ones], axis=1), NN)
    carry = jnp.zeros((owners, 128), F32)
    for b in range(blocks):
        part = ranks[b * owners : (b + 1) * owners]
        mine = own[:, b * 128 : (b + 1) * 128]
        p_scr[:, b * 128 : (b + 1) * 128] = jnp.sum(
            jnp.where(mine, part[:, :128] + carry, 0.0), axis=0, keepdims=True
        ).astype(I32)
        carry = carry + part[:, 128:]
    num_ref[...] = jnp.minimum(carry, float(CAP)).astype(I32)
    over = jnp.max(carry) > float(CAP)

    lane_out = jnp.zeros((5 * owners, CAP), F32)
    col_out = jnp.zeros((CAP, 2 * owners), F32)
    counts = jnp.zeros((128, 128), F32)
    step = 512
    for c in range(edges // step):
        at = slice(c * step, (c + 1) * step)
        sc = s_ref[:, at]
        dc = d_ref[:, at]
        bc = b_ref[:, at]
        pc = p_scr[:, at]
        okc = dc < rows_all
        low = _hot(_iota((128, step), 0) == (sc & 127))
        found = _dot(table, low, NN)
        high = _iota((128, step), 0) == (sc >> 7)
        q_hi = jnp.sum(jnp.where(high, found[:128], 0.0), axis=0, keepdims=True)
        q_lo = jnp.sum(jnp.where(high, found[128:], 0.0), axis=0, keepdims=True)
        mine = own[:, at]
        back = jnp.maximum(rows_all - 1 - dc, 0)
        values = [q_hi, q_lo, (back >> 8).astype(F32), (back & 255).astype(F32), (bc + 16).astype(F32)]
        spread = jnp.concatenate([jnp.where(mine, v, 0.0) for v in values], axis=0).astype(BF16)
        place = _hot(_iota((CAP, step), 0) == pc)
        lane_out += _dot(spread, place, NT)
        col_out += _dot(place, spread[2 * owners : 4 * owners], NT)
        d_hi = _hot((_iota((128, step), 0) == (dc >> 7)) & okc)
        d_lo = _hot(_iota((128, step), 0) == (dc & 127))
        counts += _dot(d_hi, d_lo, NT)
    filled = lane_out[4 * owners :] > 8.0
    asked = lane_out[:owners] * 256.0 + lane_out[owners : 2 * owners]
    asked = jnp.where(filled, asked, 2048.0)
    req_ref[...] = jnp.where(over, 4096.0, asked).astype(I32)
    target = lane_out[2 * owners : 3 * owners] * 256.0 + lane_out[3 * owners : 4 * owners]
    dst_ref[...] = (float(rows_all - 1) - target).astype(I32)
    bkt_ref[...] = jnp.where(filled, lane_out[4 * owners :] - 16.0, -1.0).astype(I32)
    dcol_ref[...] = float(rows_all - 1) - (col_out[:, :owners] * 256.0 + col_out[:, owners:])
    cnt_ref[...] = counts


def _serve_kernel(req_ref, feat_ref, out_ref, flag_ref):
    peers = req_ref.shape[0]
    wide = jnp.concatenate([feat_ref[i * 512 : (i + 1) * 512, :] for i in range(4)], axis=1)
    req = req_ref[...]
    flag_ref[...] = jnp.broadcast_to(jnp.max(jnp.where(req >= 4096, 1.0, 0.0), keepdims=True), flag_ref.shape)
    cols = jnp.transpose(req.astype(F32)).astype(I32)
    for r in range(peers):
        col = cols[:, r : r + 1]
        hot = _hot(_iota((CAP, 512), 1) == (col & 511))
        got = _dot(hot, wide, NN)
        part = col >> 9
        rows = jnp.where(part == 0, got[:, :128], 0.0)
        for i in range(1, 4):
            rows = jnp.where(part == i, got[:, i * 128 : (i + 1) * 128], rows)
        out_ref[r] = rows.astype(BF16)


def _kernel_parts(kern):
    high = kern.astype(BF16)
    low = (kern - high.astype(F32)).astype(BF16)
    return jnp.concatenate([high, low], axis=0)


def _kernel_rows(bkt_row, parts):
    hot = _hot(_iota((16, bkt_row.shape[1]), 0) == bkt_row)
    return _dot(jnp.concatenate([hot, hot], axis=0), parts, TN)


def _scatter_kernel(
    me_s, dst_s, num_s, rows_ref, dst_ref, bkt_ref, dcol_ref, kern_ref, cnt_ref, flag_ref, other_ref, own_ref, acc, msg
):
    owners = rows_ref.shape[0]
    chunks = own_ref.shape[0]
    node_rows = own_ref.shape[1] - EXTRA

    def clear(i, c):
        acc[pl.ds(pl.multiple_of(i * 256, 256), 256), :] = jnp.zeros((256, 128), F32)
        return c

    lax.fori_loop(0, acc.shape[0] // 256, clear, 0)
    parts = _kernel_parts(kern_ref[...])
    together = (_iota((CAP, CAP), 0) // BATCH) == (_iota((CAP, CAP), 1) // BATCH)
    for o in range(owners):
        bkt = bkt_ref[o : o + 1, :]
        m = _kernel_rows(bkt, parts) * rows_ref[o].astype(F32)
        high = m.astype(BF16)
        low = (m - high.astype(F32)).astype(BF16)
        drow = dst_ref[o : o + 1, :].astype(F32)
        same = _hot((dcol_ref[:, o : o + 1] == drow) & together)
        sums = _dot(same, jnp.concatenate([high, low], axis=1), NN)
        msg[o * CAP : (o + 1) * CAP, :] = sums[:, :128] + sums[:, 128:]
    for o in range(owners):

        def batch(i, c):
            base = i * BATCH
            at = [dst_s[o, base + k] for k in range(BATCH)]
            new = [acc[pl.ds(at[k], 1), :] + msg[pl.ds(o * CAP + base + k, 1), :] for k in range(BATCH)]
            for k in range(BATCH):
                acc[pl.ds(at[k], 1), :] = new[k]
            return c

        lax.fori_loop(0, (num_s[o, 0] + BATCH - 1) // BATCH, batch, 0)
    flag = flag_ref[0:1, :]
    z = me_s[0] // 2
    core = me_s[0] % 2
    for d in range(chunks):
        for ref, side in ((other_ref, 1 - core), (own_ref, core)):
            chunk = lax.rem(z + d, chunks) * 2 + side

            def down(i, s):
                to = pl.multiple_of(i * 256, 256)
                at = pl.multiple_of(chunk * node_rows + i * 256, 256)
                ref[d, pl.ds(to, 256), :] = acc[pl.ds(at, 256), :].astype(ref.dtype)
                return s

            lax.fori_loop(0, node_rows // 256, down, 0)
            cnt = cnt_ref[pl.ds(pl.multiple_of(chunk * 16, 16), 16), :].astype(I32)
            digits = [cnt & 31, (cnt >> 5) & 31, cnt >> 10]
            for j, digit in enumerate(digits):
                ref[d, node_rows + 16 * j : node_rows + 16 * (j + 1), :] = digit.astype(F32).astype(ref.dtype)
            ref[d, node_rows + 48 : node_rows + 64, :] = jnp.broadcast_to(flag, (16, 128)).astype(ref.dtype)


def _dense_kernel(own_ref, core_ref, up_a_ref, up_b_ref, down_a_ref, down_b_ref, feat_ref, cot_ref, ws_ref, wn_ref, out_ref, pg_ref, mean_ref, mg_ref):
    node_rows = feat_ref.shape[0]
    half = up_a_ref.shape[0]

    def summed(start, size):
        total = own_ref[start : start + size, :] + core_ref[start : start + size, :].astype(F32)
        first, second, at = (up_a_ref, down_a_ref, start) if start < half else (up_b_ref, down_b_ref, start - half)
        return total + first[at : at + size, :].astype(F32) + second[at : at + size, :].astype(F32)

    digit = [summed(node_rows + 16 * j, 16) for j in range(3)]
    degree = digit[0] + 32.0 * digit[1] + 1024.0 * digit[2]
    div_cols = jnp.transpose(jnp.maximum(degree, 1.0))
    both = jnp.concatenate([ws_ref[...], wn_ref[...]], axis=0)
    wn = wn_ref[...]
    for i in range(node_rows // 128):
        at = slice(i * 128, (i + 1) * 128)
        div = div_cols[:, i : i + 1]
        mean = (summed(i * 128, 128) / div).astype(BF16)
        z = _dot(jnp.concatenate([feat_ref[at, :], mean], axis=1), both, NN)
        sig = jax.nn.sigmoid(z)
        pg = (cot_ref[at, :].astype(F32) * sig * (1.0 + z * (1.0 - sig))).astype(BF16)
        out_ref[at, :] = (z * sig).astype(BF16)
        pg_ref[at, :] = pg
        mean_ref[at, :] = mean
        mg_ref[at, :] = (_dot(pg, wn, NT) / div).astype(BF16)


def _edge_grad_kernel(places, me_s, dst_s, num_s, rows_ref, bkt_ref, kern_ref, *refs):
    owners = rows_ref.shape[0]
    out_ref, kg_ref, table, got = refs[len(places) :]
    z = me_s[0] // 2
    core = me_s[0] % 2
    zs = table.shape[0] // 4096
    for ref, (d, other, start) in zip(refs, places):
        chunk = lax.rem(z + d, zs) * 2 + (1 - core if other else core)

        def widen(i, c):
            at = pl.multiple_of(chunk * 2048 + start + i * 256, 256)
            table[pl.ds(at, 256), :] = ref[pl.ds(pl.multiple_of(i * 256, 256), 256), :].astype(F32)
            return c

        lax.fori_loop(0, ref.shape[0] // 256, widen, 0)
    got[...] = jnp.zeros(got.shape, F32)
    for o in range(owners):

        def batch(i, c):
            base = i * BATCH
            for k in range(BATCH):
                got[pl.ds(o * CAP + base + k, 1), :] = table[pl.ds(dst_s[o, base + k], 1), :]
            return c

        lax.fori_loop(0, (num_s[o, 0] + BATCH - 1) // BATCH, batch, 0)
    parts = _kernel_parts(kern_ref[...])
    total = jnp.zeros((16, 128), F32)
    for o in range(owners):
        bkt = bkt_ref[o : o + 1, :]
        g = got[o * CAP : (o + 1) * CAP, :]
        out_ref[o] = (_kernel_rows(bkt, parts) * g).astype(BF16)
        hot = _hot(_iota((16, CAP), 0) == bkt)
        total += _dot(hot, (g * rows_ref[o].astype(F32)).astype(BF16), NN)
    kg_ref[...] = total


def _collect_kernel(req_ref, part_ref, dense_ref, out_ref):
    peers = req_ref.shape[0]
    node_rows = dense_ref.shape[0]
    step = 512
    for i in range(node_rows // step):
        at = slice(i * step, (i + 1) * step)
        total = dense_ref[at, :]
        for r in range(peers):
            hot = _hot(_iota((step, CAP), 0) + i * step == req_ref[r : r + 1, :])
            total = total + _dot(hot, part_ref[r], NN)
        out_ref[at, :] = total


VM = pl.BlockSpec(memory_space=pltpu.VMEM)
SM = pl.BlockSpec(memory_space=pltpu.SMEM)


def _call(kernel, out_shape, in_specs, scratch=(), flops=0, name=None):
    return pl.pallas_call(
        kernel,
        out_shape=out_shape,
        in_specs=in_specs,
        out_specs=jax.tree.map(lambda _: VM, out_shape),
        scratch_shapes=list(scratch),
        compiler_params=pltpu.CompilerParams(vmem_limit_bytes=48 * 1024 * 1024),
        cost_estimate=pl.CostEstimate(flops=flops, bytes_accessed=4 << 20, transcendentals=0),
        name=name,
    )


def _all_sum(x):
    for axis, step, count in (("col", 2, 4), ("col", 1, 2), ("row", 1, 4), ("row", 4, 4)):
        size = lax.axis_size(axis)
        terms = [x]
        for k in range(1, count):
            terms.append(lax.ppermute(x, axis, [(i, i ^ (k * step)) for i in range(size)]))
        while len(terms) > 1:
            terms = [terms[i] + terms[i + 1] for i in range(0, len(terms), 2)]
        x = terms[0]
    return x


def _sibling(x):
    return lax.ppermute(x, "col", [(i, i ^ 1) for i in range(lax.axis_size("col"))])


def _along_z(x, step):
    size = lax.axis_size("col")
    return lax.ppermute(x, "col", [(i, (i + 2 * step) % size) for i in range(size)])


def _reduce_chunks(other, own, half):
    sums = {}
    crossed = {}
    for d in (2, 1, 3, 0):
        crossed[d] = _sibling(other[d])
    for d in (2, 1, 3):
        sums[d] = own[d] + crossed[d].astype(F32)
    far_a = _along_z(sums[2][:half].astype(BF16), 1)
    far_b = _along_z(sums[2][half:].astype(BF16), -1)
    up_b = _along_z(sums[1][half:].astype(BF16), 1)
    down_a = _along_z(sums[3][:half].astype(BF16), -1)
    up_a = _along_z((sums[1][:half] + far_a.astype(F32)).astype(BF16), 1)
    down_b = _along_z((sums[3][half:] + far_b.astype(F32)).astype(BF16), -1)
    return own[0], crossed[0], up_a, up_b, down_a, down_b


def _gather_chunks(x, half):
    a, b = x[:half], x[half:]
    up_a = _along_z(a, 1)
    down_b = _along_z(b, -1)
    up_b = _along_z(b, 1)
    down_a = _along_z(a, -1)
    far_a = _along_z(up_a, 1)
    far_b = _along_z(down_b, -1)
    parts = [(0, 0, x), (3, 0, up_a), (1, half, down_b), (3, half, up_b), (1, 0, down_a), (2, 0, far_a), (2, half, far_b)]
    found = [((d, False, start), rows) for d, start, rows in parts]
    found += [((d, True, start), _sibling(rows)) for d, start, rows in parts]
    return found


def _general(features, cotangent, self_weight, neigh_weight, kernel, needed, src_slot, dst_local, bucket):
    row_count = lax.axis_size("row")
    col_count = lax.axis_size("col")
    node_rows = features.shape[0]
    channels = features.shape[1]
    wanted = needed.reshape(row_count, -1)
    capacity = wanted.shape[1]
    slot_ids = src_slot.reshape(-1)
    dest_ids = dst_local.reshape(-1)
    bucket_ids = bucket.reshape(-1)
    block_rows = col_count * node_rows
    one_hot = (bucket_ids[:, None] == jnp.arange(kernel.shape[0], dtype=I32)[None, :]).astype(F32)
    kernel_rows = jnp.dot(one_hot, kernel, precision=lax.Precision.HIGHEST, preferred_element_type=F32)
    gathered = lax.all_gather(features, "row", axis=0, tiled=True)
    gathered_index = slot_ids // capacity * node_rows + wanted.reshape(-1)[slot_ids]
    source_float = gathered[gathered_index].astype(F32)
    messages = kernel_rows * source_float
    summed_part = jax.ops.segment_sum(messages, dest_ids, num_segments=block_rows + 1)[:-1]
    count_part = jax.ops.segment_sum(jnp.ones(dest_ids.shape, F32), dest_ids, num_segments=block_rows + 1)[:-1]
    summed = lax.psum_scatter(summed_part, "col", scatter_dimension=0, tiled=True)
    degree = lax.psum_scatter(count_part, "col", scatter_dimension=0, tiled=True)
    divisor = jnp.maximum(degree, 1.0)[:, None]
    mean = (summed / divisor).astype(BF16)
    preact = jnp.dot(features, self_weight, preferred_element_type=F32) + jnp.dot(
        mean, neigh_weight, preferred_element_type=F32
    )
    sigmoid_z = jax.nn.sigmoid(preact)
    out_rows = (preact * sigmoid_z).astype(BF16)
    pre_grad = (cotangent.astype(F32) * sigmoid_z * (1.0 + preact * (1.0 - sigmoid_z))).astype(BF16)
    self_part = _dot(features, pre_grad, TN)
    neigh_part = _dot(mean, pre_grad, TN)
    mean_grad = (_dot(pre_grad, neigh_weight, NT) / divisor).astype(BF16)
    self_grad, neigh_grad = lax.psum((self_part, neigh_part), ("row", "col"))
    block_grad = lax.all_gather(mean_grad, "col", axis=0, tiled=True)
    padded = jnp.concatenate([block_grad, jnp.zeros((1, channels), BF16)], axis=0)
    dest_rows = padded[dest_ids].astype(F32)
    kernel_part = lax.dot_general(
        one_hot, dest_rows * source_float, TN, precision=lax.Precision.HIGHEST, preferred_element_type=F32
    )
    source_part = jax.ops.segment_sum(kernel_rows * dest_rows, gathered_index, num_segments=row_count * node_rows)
    neigh_dx = lax.psum_scatter(source_part.astype(BF16), "row", scatter_dimension=0, tiled=True).astype(F32)
    feature_grad = _dot(pre_grad, self_weight, NT) + neigh_dx
    kernel_grad = lax.psum(kernel_part, ("row", "col"))
    return (out_rows, feature_grad, self_grad, neigh_grad, kernel_grad)


def _shape(shape, dtype):
    return jax.ShapeDtypeStruct(shape, dtype)


def per_device(features, cotangent, self_weight, neigh_weight, kernel, needed, src_slot, dst_local, bucket):
    rows = lax.axis_size("row")
    cols = lax.axis_size("col")
    nodes = features.shape[0]
    edges = src_slot.shape[-1]
    line = (1, edges)
    req, dst, bkt, dcol, num, cnt = _call(
        _plan_kernel,
        (
            _shape((rows, CAP), I32),
            _shape((rows, CAP), I32),
            _shape((rows, CAP), I32),
            _shape((CAP, rows), F32),
            _shape((rows, 128), I32),
            _shape((128, 128), F32),
        ),
        [VM] * 4,
        [pltpu.VMEM((1, edges), I32)],
        name="plan",
    )(src_slot.reshape(line), dst_local.reshape(line), bucket.reshape(line), needed.reshape(128, 128))
    asked = lax.all_to_all(req, "row", 0, 0, tiled=True)
    served, flag = _call(
        _serve_kernel,
        (_shape((rows, CAP, 128), BF16), _shape((8, 128), F32)),
        [VM] * 2,
        name="serve",
    )(asked, features)
    source = lax.all_to_all(served, "row", 0, 0, tiled=True)
    me = lax.axis_index("col").astype(I32).reshape(1)
    half = nodes // 2
    other, own_sums = _call(
        _scatter_kernel,
        (_shape((cols // 2, nodes + EXTRA, 128), BF16), _shape((cols // 2, nodes + EXTRA, 128), F32)),
        [SM, SM, SM] + [VM] * 7,
        [pltpu.VMEM((cols * nodes, 128), F32), pltpu.VMEM((rows * CAP, 128), F32)],
        name="scatter",
    )(me, dst, num, source, dst, bkt, dcol, kernel, cnt, flag)
    sums = _reduce_chunks(other, own_sums, half)

    def short(args):
        features, cotangent, self_weight, neigh_weight, kernel, sums, asked, source, dst, num, bkt = args
        out_rows, pre_grad, mean, mean_grad = _call(
            _dense_kernel, tuple([_shape((nodes, 128), BF16)] * 4), [VM] * 10, name="dense"
        )(*sums, features, cotangent, self_weight, neigh_weight)
        found = _gather_chunks(mean_grad, half)
        places = [place for place, _ in found]
        grads = _dot(jnp.concatenate([features, mean], axis=1), pre_grad, TN)
        own = _dot(pre_grad, self_weight, NT)
        grads = _all_sum(grads)
        sent, kernel_part = _call(
            functools.partial(_edge_grad_kernel, places),
            (_shape((rows, CAP, 128), BF16), _shape((16, 128), F32)),
            [SM, SM, SM] + [VM] * (3 + len(places)),
            [pltpu.VMEM((cols * nodes, 128), F32), pltpu.VMEM((rows * CAP, 128), F32)],
            name="edge_grad",
        )(me, dst, num, source, bkt, kernel, *[rows for _, rows in found])
        back = lax.all_to_all(sent, "row", 0, 0, tiled=True)
        kernel_grad = _all_sum(kernel_part)
        feature_grad = _call(_collect_kernel, _shape((nodes, 128), F32), [VM] * 3, name="collect")(asked, back, own)
        return (out_rows, feature_grad, grads[:128], grads[128:], kernel_grad)

    def long(args):
        features, cotangent, self_weight, neigh_weight, kernel = args[:5]
        return _general(features, cotangent, self_weight, neigh_weight, kernel, needed, src_slot, dst_local, bucket)

    flags = [sums[0], sums[1], sums[3], sums[5]]
    at = [nodes + 48, nodes + 48, nodes + 48 - half, nodes + 48 - half]
    over = sum(x[i, 0].astype(F32) for x, i in zip(flags, at)) > 0
    return lax.cond(
        over,
        long,
        short,
        (features, cotangent, self_weight, neigh_weight, kernel, sums, asked, source, dst, num, bkt),
    )


def solution(mesh):
    placed = (
        P(("row", "col"), None),
        P(("row", "col"), None),
        P(),
        P(),
        P(),
        P("row", "col", None, None),
        P("row", "col", None),
        P("row", "col", None),
        P("row", "col", None),
    )
    return jax.shard_map(
        per_device,
        mesh=mesh,
        in_specs=placed,
        out_specs=(P(("row", "col"), None), P(("row", "col"), None), P(), P(), P()),
        check_vma=False,
    )
```

```python
import functools

import jax
import jax.numpy as jnp
from jax import lax
from jax.experimental import pallas as pl
from jax.experimental.pallas import tpu as pltpu
from jax.sharding import PartitionSpec as P

BF16 = jnp.bfloat16
F32 = jnp.float32
I32 = jnp.int32

CAP = 320
BATCH = 16
FETCH = 32
GROUP = 4
ROWS = 16384
EXTRA = 64
NT = (((1,), (1,)), ((), ()))
TN = (((0,), (0,)), ((), ()))
NN = (((1,), (0,)), ((), ()))


def _dot(a, b, dims):
    return lax.dot_general(a, b, dims, preferred_element_type=F32)


def _iota(shape, dim):
    return lax.broadcasted_iota(I32, shape, dim)


def _hot(mask):
    return jnp.where(mask, 1.0, 0.0).astype(BF16)


def _ask_kernel(s_ref, d_ref, need_ref, req_ref, p_ref, num_ref):
    owners = req_ref.shape[0]
    edges = s_ref.shape[1]
    blocks = edges // 128
    need = jnp.concatenate([need_ref[:, h * 128 : (h + 1) * 128] for h in range(8)], axis=0)
    table = jnp.concatenate([(need >> 8).astype(F32), (need & 255).astype(F32)], axis=0).astype(BF16)
    owner = jnp.where(d_ref[...] < ROWS, s_ref[...] >> 10, owners)
    own = _iota((owners, edges), 0) == owner
    own_hot = _hot(own)
    stacked = jnp.concatenate([own_hot[:, b * 128 : (b + 1) * 128] for b in range(blocks)], axis=0)
    before = _hot(_iota((128, 128), 0) < _iota((128, 128), 1))
    ones = jnp.ones((128, 128), BF16)
    ranks = _dot(stacked, jnp.concatenate([before, ones], axis=1), NN)
    carry = jnp.zeros((owners, 128), F32)
    for b in range(blocks):
        part = ranks[b * owners : (b + 1) * owners]
        mine = own[:, b * 128 : (b + 1) * 128]
        p_ref[:, b * 128 : (b + 1) * 128] = jnp.sum(
            jnp.where(mine, part[:, :128] + carry, 0.0), axis=0, keepdims=True
        ).astype(I32)
        carry = carry + part[:, 128:]
    num_ref[...] = jnp.minimum(carry, float(CAP)).astype(I32)
    over = jnp.max(carry) > float(CAP)

    out = jnp.zeros((3 * owners, CAP), F32)
    step = 512
    for c in range(edges // step):
        at = slice(c * step, (c + 1) * step)
        sc = s_ref[:, at]
        low = _hot(_iota((128, step), 0) == (sc & 127))
        found = _dot(table, low, NN)
        high = _iota((128, step), 0) == ((sc >> 7) & 7) * owners + (sc >> 10)
        q_hi = jnp.sum(jnp.where(high, found[:128], 0.0), axis=0, keepdims=True)
        q_lo = jnp.sum(jnp.where(high, found[128:], 0.0), axis=0, keepdims=True)
        mine = own[:, at]
        values = [q_hi, q_lo, jnp.ones((1, step), F32)]
        spread = jnp.concatenate([jnp.where(mine, v, 0.0) for v in values], axis=0).astype(BF16)
        place = _hot(_iota((CAP, step), 0) == p_ref[:, at])
        out += _dot(spread, place, NT)
    asked = jnp.where(out[2 * owners :] > 0.5, out[:owners] * 256.0 + out[owners : 2 * owners], 2048.0)
    req_ref[...] = jnp.where(over, 4096.0, asked).astype(I32)


def _slots_kernel(s_ref, d_ref, b_ref, p_ref, kern_ref, dst_ref, hot_ref, rows_ref, same_ref, cnt_ref):
    owners = dst_ref.shape[0]
    edges = s_ref.shape[1]
    lane_out = jnp.zeros((3 * owners, CAP), F32)
    col_out = jnp.zeros((CAP, 2 * owners), F32)
    counts = jnp.zeros((128, 128), F32)
    step = 512
    for c in range(edges // step):
        at = slice(c * step, (c + 1) * step)
        dc = d_ref[:, at]
        okc = dc < ROWS
        mine = _iota((owners, step), 0) == jnp.where(okc, s_ref[:, at] >> 10, owners)
        back = jnp.maximum(ROWS - 1 - dc, 0)
        values = [(back >> 8).astype(F32), (back & 255).astype(F32), (b_ref[:, at] + 1).astype(F32)]
        spread = jnp.concatenate([jnp.where(mine, v, 0.0) for v in values], axis=0).astype(BF16)
        place = _hot(_iota((CAP, step), 0) == p_ref[:, at])
        lane_out += _dot(spread, place, NT)
        col_out += _dot(place, spread[: 2 * owners], NT)
        d_hi = _hot((_iota((128, step), 0) == (dc >> 7)) & okc)
        d_lo = _hot(_iota((128, step), 0) == (dc & 127))
        counts += _dot(d_hi, d_lo, NT)
    cnt_ref[...] = counts
    drow = lane_out[:owners] * 256.0 + lane_out[owners : 2 * owners]
    dcol = col_out[:, :owners] * 256.0 + col_out[:, owners:]
    dst_ref[...] = (float(ROWS - 1) - drow).astype(I32)
    bucket = lane_out[2 * owners :].astype(I32) - 1
    kern = kern_ref[...]
    high = kern.astype(BF16)
    parts = jnp.concatenate([high, (kern - high.astype(F32)).astype(BF16)], axis=0)
    together = (_iota((CAP, CAP), 0) // BATCH) == (_iota((CAP, CAP), 1) // BATCH)
    for o in range(owners):
        hot = _hot(_iota((16, CAP), 0) == bucket[o : o + 1, :])
        hot_ref[o] = hot
        rows_ref[o] = _dot(jnp.concatenate([hot, hot], axis=0), parts, TN)
        same_ref[o] = _hot((dcol[:, o : o + 1] == drow[o : o + 1, :]) & together)


def _serve_kernel(req_ref, feat_ref, out_ref, flag_ref):
    peers = req_ref.shape[0]
    wide = jnp.concatenate([feat_ref[i * 512 : (i + 1) * 512, :] for i in range(4)], axis=1)
    req = req_ref[...]
    flag_ref[...] = jnp.broadcast_to(jnp.max(jnp.where(req >= 4096, 1.0, 0.0), keepdims=True), flag_ref.shape)
    cols = jnp.transpose(req.astype(F32)).astype(I32)
    for g in range(peers // GROUP):
        peers_of = range(g * GROUP, (g + 1) * GROUP)
        hots = [_hot(_iota((CAP, 512), 1) == (cols[:, r : r + 1] & 511)) for r in peers_of]
        got = _dot(jnp.concatenate(hots, axis=0), wide, NN)
        for k, r in enumerate(peers_of):
            part = cols[:, r : r + 1] >> 9
            mine = got[k * CAP : (k + 1) * CAP]
            rows = jnp.where(part == 0, mine[:, :128], 0.0)
            for i in range(1, 4):
                rows = jnp.where(part == i, mine[:, i * 128 : (i + 1) * 128], rows)
            out_ref[r] = rows.astype(BF16)


def _scatter_kernel(
    me_s, dst_s, num_s, rows_ref, kern_hbm, same_hbm, cnt_ref, flag_ref, other_ref, own_ref, acc, msg, kern_ref, same_ref, sems
):
    owners = rows_ref.shape[0]
    copies = [
        pltpu.make_async_copy(kern_hbm, kern_ref, sems.at[0]),
        pltpu.make_async_copy(same_hbm, same_ref, sems.at[1]),
    ]
    for copy in copies:
        copy.start()
    chunks = own_ref.shape[0]
    node_rows = own_ref.shape[1] - EXTRA

    def clear(i, c):
        acc[pl.ds(pl.multiple_of(i * 256, 256), 256), :] = jnp.zeros((256, 128), F32)
        return c

    lax.fori_loop(0, acc.shape[0] // 256, clear, 0)
    for copy in copies:
        copy.wait()
    for o in range(owners):
        m = kern_ref[o] * rows_ref[o].astype(F32)
        high = m.astype(BF16)
        low = (m - high.astype(F32)).astype(BF16)
        sums = _dot(same_ref[o], jnp.concatenate([high, low], axis=1), NN)
        msg[o * CAP : (o + 1) * CAP, :] = sums[:, :128] + sums[:, 128:]
    for o in range(owners):

        def batch(i, c):
            base = pl.multiple_of(o * CAP + i * BATCH, BATCH)
            at = [dst_s[base + k] for k in range(BATCH)]
            new = [acc[pl.ds(at[k], 1), :] + msg[pl.ds(base + k, 1), :] for k in range(BATCH)]
            for k in range(BATCH):
                acc[pl.ds(at[k], 1), :] = new[k]
            return c

        lax.fori_loop(0, (num_s[o, 0] + BATCH - 1) // BATCH, batch, 0)
    flag = flag_ref[0:1, :]
    z = me_s[0] // 2
    core = me_s[0] % 2
    for d in range(chunks):
        for ref, side in ((other_ref, 1 - core), (own_ref, core)):
            chunk = lax.rem(z + d, chunks) * 2 + side

            def down(i, s):
                to = pl.multiple_of(i * 256, 256)
                at = pl.multiple_of(chunk * node_rows + i * 256, 256)
                ref[d, pl.ds(to, 256), :] = acc[pl.ds(at, 256), :].astype(ref.dtype)
                return s

            lax.fori_loop(0, node_rows // 256, down, 0)
            cnt = cnt_ref[pl.ds(pl.multiple_of(chunk * 16, 16), 16), :].astype(I32)
            digits = [cnt & 31, (cnt >> 5) & 31, cnt >> 10]
            for j, digit in enumerate(digits):
                ref[d, node_rows + 16 * j : node_rows + 16 * (j + 1), :] = digit.astype(F32).astype(ref.dtype)
            ref[d, node_rows + 48 : node_rows + 64, :] = jnp.broadcast_to(flag, (16, 128)).astype(ref.dtype)


def _dense_kernel(own_ref, core_ref, up_a_ref, up_b_ref, down_a_ref, down_b_ref, feat_ref, cot_ref, ws_ref, wn_ref, out_ref, pg_ref, mean_ref, mg_ref, flag_ref):
    node_rows = feat_ref.shape[0]
    half = up_a_ref.shape[0]

    def summed(start, size):
        total = own_ref[start : start + size, :].astype(F32) + core_ref[start : start + size, :].astype(F32)
        first, second, at = (up_a_ref, down_a_ref, start) if start < half else (up_b_ref, down_b_ref, start - half)
        return total + first[at : at + size, :].astype(F32) + second[at : at + size, :].astype(F32)

    digit = [summed(node_rows + 16 * j, 16) for j in range(3)]
    flag_ref[...] = summed(node_rows + 48, 8)
    degree = digit[0] + 32.0 * digit[1] + 1024.0 * digit[2]
    div_cols = jnp.transpose(jnp.maximum(degree, 1.0))
    both = jnp.concatenate([ws_ref[...], wn_ref[...]], axis=0)
    wn = wn_ref[...]
    for i in range(node_rows // 128):
        at = slice(i * 128, (i + 1) * 128)
        div = div_cols[:, i : i + 1]
        mean = (summed(i * 128, 128) / div).astype(BF16)
        z = _dot(jnp.concatenate([feat_ref[at, :], mean], axis=1), both, NN)
        sig = jax.nn.sigmoid(z)
        pg = (cot_ref[at, :].astype(F32) * sig * (1.0 + z * (1.0 - sig))).astype(BF16)
        out_ref[at, :] = (z * sig).astype(BF16)
        pg_ref[at, :] = pg
        mean_ref[at, :] = mean
        mg_ref[at, :] = (_dot(pg, wn, NT) / div).astype(BF16)


def _edge_grad_kernel(places, me_s, dst_s, num_s, rows_ref, hot_ref, kern_ref, *refs):
    owners = rows_ref.shape[0]
    out_ref, kg_ref, table, got = refs[len(places) :]
    z = me_s[0] // 2
    core = me_s[0] % 2
    zs = table.shape[0] // 4096
    for ref, (d, other, start) in zip(refs, places):
        chunk = lax.rem(z + d, zs) * 2 + (1 - core if other else core)

        def widen(i, c):
            at = pl.multiple_of(chunk * 2048 + start + i * 256, 256)
            table[pl.ds(at, 256), :] = ref[pl.ds(pl.multiple_of(i * 256, 256), 256), :].astype(F32)
            return c

        lax.fori_loop(0, ref.shape[0] // 256, widen, 0)
    got[...] = jnp.zeros(got.shape, F32)
    for o in range(owners):

        def batch(i, c):
            base = pl.multiple_of(o * CAP + i * FETCH, FETCH)
            at = [dst_s[base + k] for k in range(FETCH)]
            for k in range(FETCH):
                got[pl.ds(base + k, 1), :] = table[pl.ds(at[k], 1), :]
            return c

        lax.fori_loop(0, (num_s[o, 0] + FETCH - 1) // FETCH, batch, 0)
    total = jnp.zeros((16, 128), F32)
    for o in range(owners):
        g = got[o * CAP : (o + 1) * CAP, :]
        out_ref[o] = (kern_ref[o] * g).astype(BF16)
        total += _dot(hot_ref[o], (g * rows_ref[o].astype(F32)).astype(BF16), NN)
    kg_ref[...] = total


def _collect_kernel(req_ref, line_ref, part_ref, dense_ref, out_ref):
    peers = req_ref.shape[0]
    cols = jnp.transpose(req_ref[...].astype(F32)).astype(I32) >> 9
    total = jnp.concatenate([dense_ref[i * 512 : (i + 1) * 512, :] for i in range(4)], axis=1)
    wide = GROUP * CAP
    for g in range(peers // GROUP):
        hots = _hot(_iota((512, wide), 0) == (line_ref[:, g * wide : (g + 1) * wide] & 511))
        spread = []
        for r in range(g * GROUP, (g + 1) * GROUP):
            rows = part_ref[r].astype(F32)
            block = cols[:, r : r + 1]
            spread.append(jnp.concatenate([jnp.where(block == i, rows, 0.0).astype(BF16) for i in range(4)], axis=1))
        total = total + _dot(hots, jnp.concatenate(spread, axis=0), NN)
    for i in range(4):
        out_ref[i * 512 : (i + 1) * 512, :] = total[:, i * 128 : (i + 1) * 128]


VM = pl.BlockSpec(memory_space=pltpu.VMEM)
SM = pl.BlockSpec(memory_space=pltpu.SMEM)
ANY = pl.BlockSpec(memory_space=pl.ANY)


def _call(kernel, out_shape, in_specs, scratch=(), limit=16, name=None):
    return pl.pallas_call(
        kernel,
        out_shape=out_shape,
        in_specs=in_specs,
        out_specs=jax.tree.map(lambda _: VM, out_shape),
        scratch_shapes=list(scratch),
        compiler_params=pltpu.CompilerParams(vmem_limit_bytes=limit << 20),
        cost_estimate=pl.CostEstimate(flops=1 << 31, bytes_accessed=4 << 20, transcendentals=0),
        name=name,
    )


def _sum_over(x, dims):
    for axis, step, count in dims:
        size = lax.axis_size(axis)
        terms = [x]
        for k in range(1, count):
            terms.append(lax.ppermute(x, axis, [(i, i ^ (k * step)) for i in range(size)]))
        while len(terms) > 1:
            terms = [terms[i] + terms[i + 1] for i in range(0, len(terms), 2)]
        x = terms[0]
    return x


OVER_COL = (("col", 2, 4), ("col", 1, 2))
OVER_ROW = (("row", 1, 4), ("row", 4, 4))


def _sibling(x):
    return lax.ppermute(x, "col", [(i, i ^ 1) for i in range(lax.axis_size("col"))])


def _along_z(x, step):
    size = lax.axis_size("col")
    return lax.ppermute(x, "col", [(i, (i + 2 * step) % size) for i in range(size)])


def _reduce_chunks(other, own, half):
    sums = {}
    crossed = {}
    for d in (2, 1, 3, 0):
        crossed[d] = _sibling(other[d])
    sums[2] = own[2].astype(F32) + crossed[2].astype(F32)
    sums[2], crossed[1], crossed[3] = lax.optimization_barrier((sums[2], crossed[1], crossed[3]))
    for d in (1, 3):
        sums[d] = own[d].astype(F32) + crossed[d].astype(F32)
    far_a = _along_z(sums[2][:half].astype(BF16), 1)
    far_b = _along_z(sums[2][half:].astype(BF16), -1)
    up_b = _along_z(sums[1][half:].astype(BF16), 1)
    down_a = _along_z(sums[3][:half].astype(BF16), -1)
    up_a = _along_z((sums[1][:half] + far_a.astype(F32)).astype(BF16), 1)
    down_b = _along_z((sums[3][half:] + far_b.astype(F32)).astype(BF16), -1)
    return own[0], crossed[0], up_a, up_b, down_a, down_b


def _gather_chunks(x, half):
    a, b = x[:half], x[half:]
    up_a = _along_z(a, 1)
    down_b = _along_z(b, -1)
    up_b = _along_z(b, 1)
    down_a = _along_z(a, -1)
    far_a = _along_z(up_a, 1)
    far_b = _along_z(down_b, -1)
    first = [_sibling(x), _sibling(up_a), _sibling(down_b)]
    up_b, down_a, *first = lax.optimization_barrier((up_b, down_a, *first))
    crossed = first + [_sibling(up_b), _sibling(down_a), _sibling(far_a), _sibling(far_b)]
    rows = [x, up_a, down_b, up_b, down_a, far_a, far_b]
    at = [(0, 0), (3, 0), (1, half), (3, half), (1, 0), (2, 0), (2, half)]
    found = [((d, False, start), part) for (d, start), part in zip(at, rows)]
    return found + [((d, True, start), part) for (d, start), part in zip(at, crossed)]


def _general(features, cotangent, self_weight, neigh_weight, kernel, needed, src_slot, dst_local, bucket):
    row_count = lax.axis_size("row")
    col_count = lax.axis_size("col")
    node_rows = features.shape[0]
    channels = features.shape[1]
    wanted = needed.reshape(row_count, -1)
    capacity = wanted.shape[1]
    slot_ids = src_slot.reshape(-1)
    dest_ids = dst_local.reshape(-1)
    bucket_ids = bucket.reshape(-1)
    block_rows = col_count * node_rows
    one_hot = (bucket_ids[:, None] == jnp.arange(kernel.shape[0], dtype=I32)[None, :]).astype(F32)
    kernel_rows = jnp.dot(one_hot, kernel, precision=lax.Precision.HIGHEST, preferred_element_type=F32)
    gathered = lax.all_gather(features, "row", axis=0, tiled=True)
    gathered_index = slot_ids // capacity * node_rows + wanted.reshape(-1)[slot_ids]
    source_float = gathered[gathered_index].astype(F32)
    messages = kernel_rows * source_float
    summed_part = jax.ops.segment_sum(messages, dest_ids, num_segments=block_rows + 1)[:-1]
    count_part = jax.ops.segment_sum(jnp.ones(dest_ids.shape, F32), dest_ids, num_segments=block_rows + 1)[:-1]
    summed = lax.psum_scatter(summed_part, "col", scatter_dimension=0, tiled=True)
    degree = lax.psum_scatter(count_part, "col", scatter_dimension=0, tiled=True)
    divisor = jnp.maximum(degree, 1.0)[:, None]
    mean = (summed / divisor).astype(BF16)
    preact = jnp.dot(features, self_weight, preferred_element_type=F32) + jnp.dot(
        mean, neigh_weight, preferred_element_type=F32
    )
    sigmoid_z = jax.nn.sigmoid(preact)
    out_rows = (preact * sigmoid_z).astype(BF16)
    pre_grad = (cotangent.astype(F32) * sigmoid_z * (1.0 + preact * (1.0 - sigmoid_z))).astype(BF16)
    weight_part = _dot(jnp.concatenate([features, mean], axis=1), pre_grad, TN)
    mean_grad = (_dot(pre_grad, neigh_weight, NT) / divisor).astype(BF16)
    grads = lax.psum(weight_part, ("row", "col"))
    block_grad = lax.all_gather(mean_grad, "col", axis=0, tiled=True)
    padded = jnp.concatenate([block_grad, jnp.zeros((1, channels), BF16)], axis=0)
    dest_rows = padded[dest_ids].astype(F32)
    kernel_part = lax.dot_general(
        one_hot, dest_rows * source_float, TN, precision=lax.Precision.HIGHEST, preferred_element_type=F32
    )
    source_part = jax.ops.segment_sum(kernel_rows * dest_rows, gathered_index, num_segments=row_count * node_rows)
    neigh_dx = lax.psum_scatter(source_part.astype(BF16), "row", scatter_dimension=0, tiled=True).astype(F32)
    feature_grad = _dot(pre_grad, self_weight, NT) + neigh_dx
    kernel_grad = lax.psum(kernel_part, ("row", "col"))
    return (out_rows, feature_grad, grads[:128], grads[128:], kernel_grad)


def _shape(shape, dtype):
    return jax.ShapeDtypeStruct(shape, dtype)


def per_device(features, cotangent, self_weight, neigh_weight, kernel, needed, src_slot, dst_local, bucket):
    rows = lax.axis_size("row")
    cols = lax.axis_size("col")
    nodes = features.shape[0]
    edges = src_slot.shape[-1]
    line = (1, edges)
    s_line, d_line, b_line = src_slot.reshape(line), dst_local.reshape(line), bucket.reshape(line)
    req, place, num = _call(
        _ask_kernel,
        (_shape((rows, CAP), I32), _shape(line, I32), _shape((rows, 128), I32)),
        [VM] * 3,
        name="ask",
    )(s_line, d_line, needed.reshape(rows, -1))
    asked = lax.all_to_all(req, "row", 0, 0, tiled=True)
    dst, hot, kern_rows, same, cnt = _call(
        _slots_kernel,
        (
            _shape((rows, CAP), I32),
            _shape((rows, 16, CAP), BF16),
            _shape((rows, CAP, 128), F32),
            _shape((rows, CAP, CAP), BF16),
            _shape((128, 128), F32),
        ),
        [VM] * 5,
        limit=24,
        name="slots",
    )(s_line, d_line, b_line, place, kernel)
    dst = dst.reshape(-1)
    served, flag = _call(
        _serve_kernel,
        (_shape((rows, CAP, 128), BF16), _shape((8, 128), F32)),
        [VM] * 2,
        name="serve",
    )(asked, features)
    source = lax.all_to_all(served, "row", 0, 0, tiled=True)
    me = lax.axis_index("col").astype(I32).reshape(1)
    half = nodes // 2
    other, own_sums = _call(
        _scatter_kernel,
        tuple([_shape((cols // 2, nodes + EXTRA, 128), BF16)] * 2),
        [SM, SM, SM, VM, ANY, ANY, VM, VM],
        [
            pltpu.VMEM((cols * nodes, 128), F32),
            pltpu.VMEM((rows * CAP, 128), F32),
            pltpu.VMEM(kern_rows.shape, F32),
            pltpu.VMEM(same.shape, BF16),
            pltpu.SemaphoreType.DMA((2,)),
        ],
        limit=48,
        name="scatter",
    )(me, dst, num, source, kern_rows, same, cnt, flag)
    sums = _reduce_chunks(other, own_sums, half)
    out_rows, pre_grad, mean, mean_grad, over = _call(
        _dense_kernel,
        tuple([_shape((nodes, 128), BF16)] * 4) + (_shape((8, 128), F32),),
        [VM] * 10,
        name="dense",
    )(*sums, features, cotangent, self_weight, neigh_weight)
    found = _gather_chunks(mean_grad, half)
    places = [at for at, _ in found]
    weight_part = _dot(jnp.concatenate([features, mean], axis=1), pre_grad, TN)
    own = _dot(pre_grad, self_weight, NT)
    pieces = [part for _, part in found]
    sent, kernel_part = _call(
        functools.partial(_edge_grad_kernel, places),
        (_shape((rows, CAP, 128), BF16), _shape((16, 128), F32)),
        [SM, SM, SM] + [VM] * (3 + len(places)),
        [pltpu.VMEM((cols * nodes, 128), F32), pltpu.VMEM((rows * CAP, 128), F32)],
        limit=36,
        name="edge_grad",
    )(me, dst, num, source, hot, kern_rows, *pieces)
    back = lax.all_to_all(sent, "row", 0, 0, tiled=True)
    grads = _sum_over(jnp.concatenate([weight_part, kernel_part], axis=0), OVER_COL + OVER_ROW[:1])
    back, grads = lax.optimization_barrier((back, grads))
    grads = _sum_over(grads, OVER_ROW[1:])
    feature_grad = _call(_collect_kernel, _shape((nodes, 128), F32), [VM] * 4, name="collect")(
        asked, asked.reshape(1, -1), back, own
    )
    outs = (out_rows, feature_grad, grads[:128], grads[128:256], grads[256:])
    inputs = (features, cotangent, self_weight, neigh_weight, kernel, needed, src_slot, dst_local, bucket)
    state = lax.while_loop(
        lambda state: state[0], lambda state: (jnp.zeros((), bool), _general(*inputs)), (over[0, 0] > 0, outs)
    )
    return state[1]


def solution(mesh):
    placed = (
        P(("row", "col"), None),
        P(("row", "col"), None),
        P(),
        P(),
        P(),
        P("row", "col", None, None),
        P("row", "col", None),
        P("row", "col", None),
        P("row", "col", None),
    )
    return jax.shard_map(
        per_device,
        mesh=mesh,
        in_specs=placed,
        out_specs=(P(("row", "col"), None), P(("row", "col"), None), P(), P(), P()),
        check_vma=False,
    )
```

```python
import functools

import jax
import jax.numpy as jnp
from jax import lax
from jax.experimental import pallas as pl
from jax.experimental.pallas import tpu as pltpu
from jax.sharding import PartitionSpec as P

BF16 = jnp.bfloat16
F32 = jnp.float32
I32 = jnp.int32

CAP = 320
BATCH = 16
FETCH = 32
GROUP = 4
ROWS = 16384
EXTRA = 64
NT = (((1,), (1,)), ((), ()))
TN = (((0,), (0,)), ((), ()))
NN = (((1,), (0,)), ((), ()))


def _dot(a, b, dims):
    return lax.dot_general(a, b, dims, preferred_element_type=F32)


def _iota(shape, dim):
    return lax.broadcasted_iota(I32, shape, dim)


def _hot(mask):
    return jnp.where(mask, 1.0, 0.0).astype(BF16)


def _ask_kernel(s_ref, d_ref, need_ref, req_ref, p_ref, num_ref):
    owners = req_ref.shape[0]
    edges = s_ref.shape[1]
    blocks = edges // 128
    need = jnp.concatenate([need_ref[:, h * 128 : (h + 1) * 128] for h in range(8)], axis=0)
    table = jnp.concatenate([(need >> 8).astype(F32), (need & 255).astype(F32)], axis=0).astype(BF16)
    owner = jnp.where(d_ref[...] < ROWS, s_ref[...] >> 10, owners)
    own = _iota((owners, edges), 0) == owner
    own_hot = _hot(own)
    stacked = jnp.concatenate([own_hot[:, b * 128 : (b + 1) * 128] for b in range(blocks)], axis=0)
    before = _hot(_iota((128, 128), 0) < _iota((128, 128), 1))
    ones = jnp.ones((128, 128), BF16)
    ranks = _dot(stacked, jnp.concatenate([before, ones], axis=1), NN)
    carry = jnp.zeros((owners, 128), F32)
    for b in range(blocks):
        part = ranks[b * owners : (b + 1) * owners]
        mine = own[:, b * 128 : (b + 1) * 128]
        p_ref[:, b * 128 : (b + 1) * 128] = jnp.sum(
            jnp.where(mine, part[:, :128] + carry, 0.0), axis=0, keepdims=True
        ).astype(I32)
        carry = carry + part[:, 128:]
    num_ref[...] = jnp.minimum(carry, float(CAP)).astype(I32)
    over = jnp.max(carry) > float(CAP)

    out = jnp.zeros((3 * owners, CAP), F32)
    step = 512
    for c in range(edges // step):
        at = slice(c * step, (c + 1) * step)
        sc = s_ref[:, at]
        low = _hot(_iota((128, step), 0) == (sc & 127))
        found = _dot(table, low, NN)
        high = _iota((128, step), 0) == ((sc >> 7) & 7) * owners + (sc >> 10)
        q_hi = jnp.sum(jnp.where(high, found[:128], 0.0), axis=0, keepdims=True)
        q_lo = jnp.sum(jnp.where(high, found[128:], 0.0), axis=0, keepdims=True)
        mine = own[:, at]
        values = [q_hi, q_lo, jnp.ones((1, step), F32)]
        spread = jnp.concatenate([jnp.where(mine, v, 0.0) for v in values], axis=0).astype(BF16)
        place = _hot(_iota((CAP, step), 0) == p_ref[:, at])
        out += _dot(spread, place, NT)
    asked = jnp.where(out[2 * owners :] > 0.5, out[:owners] * 256.0 + out[owners : 2 * owners], 2048.0)
    req_ref[...] = jnp.where(over, 4096.0, asked).astype(I32)


def _slots_kernel(s_ref, d_ref, b_ref, p_ref, dst_ref, hot_ref, same_ref, cnt_ref):
    owners = dst_ref.shape[0]
    edges = s_ref.shape[1]
    lane_out = jnp.zeros((3 * owners, CAP), F32)
    col_out = jnp.zeros((CAP, 2 * owners), F32)
    counts = jnp.zeros((128, 128), F32)
    step = 512
    for c in range(edges // step):
        at = slice(c * step, (c + 1) * step)
        dc = d_ref[:, at]
        okc = dc < ROWS
        mine = _iota((owners, step), 0) == jnp.where(okc, s_ref[:, at] >> 10, owners)
        back = jnp.maximum(ROWS - 1 - dc, 0)
        values = [(back >> 8).astype(F32), (back & 255).astype(F32), (b_ref[:, at] + 1).astype(F32)]
        spread = jnp.concatenate([jnp.where(mine, v, 0.0) for v in values], axis=0).astype(BF16)
        place = _hot(_iota((CAP, step), 0) == p_ref[:, at])
        lane_out += _dot(spread, place, NT)
        col_out += _dot(place, spread[: 2 * owners], NT)
        d_hi = _hot((_iota((128, step), 0) == (dc >> 7)) & okc)
        d_lo = _hot(_iota((128, step), 0) == (dc & 127))
        counts += _dot(d_hi, d_lo, NT)
    cnt_ref[...] = counts
    drow = lane_out[:owners] * 256.0 + lane_out[owners : 2 * owners]
    dcol = col_out[:, :owners] * 256.0 + col_out[:, owners:]
    dst_ref[...] = (float(ROWS - 1) - drow).astype(I32)
    bucket = lane_out[2 * owners :].astype(I32) - 1
    together = (_iota((CAP, CAP), 0) // BATCH) == (_iota((CAP, CAP), 1) // BATCH)
    for o in range(owners):
        hot_ref[o] = _hot(_iota((16, CAP), 0) == bucket[o : o + 1, :])
        same_ref[o] = _hot((dcol[:, o : o + 1] == drow[o : o + 1, :]) & together)


def _serve_kernel(req_ref, feat_ref, out_ref, flag_ref):
    peers = req_ref.shape[0]
    wide = jnp.concatenate([feat_ref[i * 512 : (i + 1) * 512, :] for i in range(4)], axis=1)
    req = req_ref[...]
    flag_ref[...] = jnp.broadcast_to(jnp.max(jnp.where(req >= 4096, 1.0, 0.0), keepdims=True), flag_ref.shape)
    cols = jnp.transpose(req.astype(F32)).astype(I32)
    for g in range(peers // GROUP):
        peers_of = range(g * GROUP, (g + 1) * GROUP)
        hots = [_hot(_iota((CAP, 512), 1) == (cols[:, r : r + 1] & 511)) for r in peers_of]
        got = _dot(jnp.concatenate(hots, axis=0), wide, NN)
        for k, r in enumerate(peers_of):
            part = cols[:, r : r + 1] >> 9
            mine = got[k * CAP : (k + 1) * CAP]
            rows = jnp.where(part == 0, mine[:, :128], 0.0)
            for i in range(1, 4):
                rows = jnp.where(part == i, mine[:, i * 128 : (i + 1) * 128], rows)
            out_ref[r] = rows.astype(BF16)


def _kernel_parts(kern):
    high = kern.astype(BF16)
    return jnp.concatenate([high, (kern - high.astype(F32)).astype(BF16)], axis=0)


def _kernel_rows(hot, parts):
    return _dot(jnp.concatenate([hot, hot], axis=0), parts, TN)


def _scatter_kernel(
    me_s, dst_s, num_s, rows_ref, hot_ref, kern_ref, same_hbm, cnt_ref, flag_ref, other_ref, own_ref, acc, msg, same_ref, sem
):
    owners = rows_ref.shape[0]
    copy = pltpu.make_async_copy(same_hbm, same_ref, sem)
    copy.start()
    parts = _kernel_parts(kern_ref[...])
    chunks = own_ref.shape[0]
    node_rows = own_ref.shape[1] - EXTRA

    def clear(i, c):
        acc[pl.ds(pl.multiple_of(i * 256, 256), 256), :] = jnp.zeros((256, 128), F32)
        return c

    lax.fori_loop(0, acc.shape[0] // 256, clear, 0)
    copy.wait()
    for o in range(owners):
        m = _kernel_rows(hot_ref[o], parts) * rows_ref[o].astype(F32)
        high = m.astype(BF16)
        low = (m - high.astype(F32)).astype(BF16)
        sums = _dot(same_ref[o], jnp.concatenate([high, low], axis=1), NN)
        msg[o * CAP : (o + 1) * CAP, :] = sums[:, :128] + sums[:, 128:]
    for o in range(owners):

        def batch(i, c):
            base = pl.multiple_of(o * CAP + i * BATCH, BATCH)
            at = [dst_s[base + k] for k in range(BATCH)]
            new = [acc[pl.ds(at[k], 1), :] + msg[pl.ds(base + k, 1), :] for k in range(BATCH)]
            for k in range(BATCH):
                acc[pl.ds(at[k], 1), :] = new[k]
            return c

        lax.fori_loop(0, (num_s[o, 0] + BATCH - 1) // BATCH, batch, 0)
    flag = flag_ref[0:1, :]
    z = me_s[0] // 2
    core = me_s[0] % 2
    for d in range(chunks):
        for ref, side in ((other_ref.at[d], 1 - core), (own_ref.at[d], core)):
            chunk = lax.rem(z + d, chunks) * 2 + side

            def down(i, s):
                to = pl.multiple_of(i * 256, 256)
                at = pl.multiple_of(chunk * node_rows + i * 256, 256)
                ref[pl.ds(to, 256), :] = acc[pl.ds(at, 256), :].astype(ref.dtype)
                return s

            lax.fori_loop(0, node_rows // 256, down, 0)
            cnt = cnt_ref[pl.ds(pl.multiple_of(chunk * 16, 16), 16), :].astype(I32)
            digits = [cnt & 31, (cnt >> 5) & 31, cnt >> 10]
            for j, digit in enumerate(digits):
                ref[node_rows + 16 * j : node_rows + 16 * (j + 1), :] = digit.astype(F32).astype(ref.dtype)
            ref[node_rows + 48 : node_rows + 64, :] = jnp.broadcast_to(flag, (16, 128)).astype(ref.dtype)


def _dense_kernel(own_ref, core_ref, up_a_ref, up_b_ref, down_a_ref, down_b_ref, feat_ref, cot_ref, ws_ref, wn_ref, out_ref, pg_ref, mean_ref, mg_ref, flag_ref):
    node_rows = feat_ref.shape[0]
    half = up_a_ref.shape[0]

    def summed(start, size):
        total = own_ref[start : start + size, :].astype(F32) + core_ref[start : start + size, :].astype(F32)
        first, second, at = (up_a_ref, down_a_ref, start) if start < half else (up_b_ref, down_b_ref, start - half)
        return total + first[at : at + size, :].astype(F32) + second[at : at + size, :].astype(F32)

    digit = [summed(node_rows + 16 * j, 16) for j in range(3)]
    flag_ref[...] = summed(node_rows + 48, 8)
    degree = digit[0] + 32.0 * digit[1] + 1024.0 * digit[2]
    div_cols = jnp.transpose(jnp.maximum(degree, 1.0))
    both = jnp.concatenate([ws_ref[...], wn_ref[...]], axis=0)
    wn = wn_ref[...]
    for i in range(node_rows // 128):
        at = slice(i * 128, (i + 1) * 128)
        div = div_cols[:, i : i + 1]
        mean = (summed(i * 128, 128) / div).astype(BF16)
        z = _dot(jnp.concatenate([feat_ref[at, :], mean], axis=1), both, NN)
        sig = jax.nn.sigmoid(z)
        pg = (cot_ref[at, :].astype(F32) * sig * (1.0 + z * (1.0 - sig))).astype(BF16)
        out_ref[at, :] = (z * sig).astype(BF16)
        pg_ref[at, :] = pg
        mean_ref[at, :] = mean
        mg_ref[at, :] = (_dot(pg, wn, NT) / div).astype(BF16)


def _weights_kernel(place_s, feat_ref, mean_ref, pg_ref, *share_refs):
    pg = pg_ref[...]
    parts = [_dot(feat_ref[...], pg, TN), _dot(mean_ref[...], pg, TN)]
    rows = share_refs[0].shape[0]
    quarters = [part[i * rows : (i + 1) * rows] for part in parts for i in range(2)]
    for k, ref in enumerate(share_refs):
        which = place_s[0] ^ k
        share = quarters[0]
        for j in range(1, 4):
            share = jnp.where(which == j, quarters[j], share)
        ref[...] = share


def _edge_grad_kernel(places, me_s, dst_s, num_s, rows_ref, hot_ref, kern_ref, *refs):
    owners = rows_ref.shape[0]
    out_ref, sum_ref, table, got = refs[len(places) :]
    z = me_s[0] // 2
    core = me_s[0] % 2
    zs = table.shape[0] // 4096
    for ref, (d, other, start) in zip(refs, places):
        chunk = lax.rem(z + d, zs) * 2 + (1 - core if other else core)

        def widen(i, c):
            at = pl.multiple_of(chunk * 2048 + start + i * 256, 256)
            table[pl.ds(at, 256), :] = ref[pl.ds(pl.multiple_of(i * 256, 256), 256), :].astype(F32)
            return c

        lax.fori_loop(0, ref.shape[0] // 256, widen, 0)
    got[...] = jnp.zeros(got.shape, F32)
    for o in range(owners):

        def batch(i, c):
            base = pl.multiple_of(o * CAP + i * FETCH, FETCH)
            at = [dst_s[base + k] for k in range(FETCH)]
            for k in range(FETCH):
                got[pl.ds(base + k, 1), :] = table[pl.ds(at[k], 1), :]
            return c

        lax.fori_loop(0, (num_s[o, 0] + FETCH - 1) // FETCH, batch, 0)
    parts = _kernel_parts(kern_ref[...])
    total = jnp.zeros((16, 128), F32)
    for o in range(owners):
        g = got[o * CAP : (o + 1) * CAP, :]
        out_ref[o] = (_kernel_rows(hot_ref[o], parts) * g).astype(BF16)
        total += _dot(hot_ref[o], (g * rows_ref[o].astype(F32)).astype(BF16), NN)
    sum_ref[...] = total


def _join_kernel(*refs):
    shares, kern_ref, out_ref = refs[:-2], refs[-2], refs[-1]
    rows = shares[0].shape[0]
    out_ref[:rows, :] = _add([share[...] for share in shares])
    out_ref[rows:, :] = kern_ref[...]


def _collect_kernel(req_ref, line_ref, part_ref, dense_ref, out_ref):
    peers = req_ref.shape[0]
    cols = jnp.transpose(req_ref[...].astype(F32)).astype(I32) >> 9
    total = jnp.concatenate([dense_ref[i * 512 : (i + 1) * 512, :] for i in range(4)], axis=1)
    wide = GROUP * CAP
    for g in range(peers // GROUP):
        hots = _hot(_iota((512, wide), 0) == (line_ref[:, g * wide : (g + 1) * wide] & 511))
        spread = []
        for r in range(g * GROUP, (g + 1) * GROUP):
            rows = part_ref[r].astype(F32)
            block = cols[:, r : r + 1]
            spread.append(jnp.concatenate([jnp.where(block == i, rows, 0.0).astype(BF16) for i in range(4)], axis=1))
        total = total + _dot(hots, jnp.concatenate(spread, axis=0), NN)
    for i in range(4):
        out_ref[i * 512 : (i + 1) * 512, :] = total[:, i * 128 : (i + 1) * 128]


VM = pl.BlockSpec(memory_space=pltpu.VMEM)
SM = pl.BlockSpec(memory_space=pltpu.SMEM)
ANY = pl.BlockSpec(memory_space=pl.ANY)


def _call(kernel, out_shape, in_specs, scratch=(), limit=16, flops=1 << 31, name=None):
    return pl.pallas_call(
        kernel,
        out_shape=out_shape,
        in_specs=in_specs,
        out_specs=jax.tree.map(lambda _: VM, out_shape),
        scratch_shapes=list(scratch),
        compiler_params=pltpu.CompilerParams(vmem_limit_bytes=limit << 20),
        cost_estimate=pl.CostEstimate(flops=flops, bytes_accessed=4 << 20, transcendentals=0),
        name=name,
    )


def _exchange(x, axis, step, count):
    size = lax.axis_size(axis)
    return [x] + [lax.ppermute(x, axis, [(i, i ^ (k * step)) for i in range(size)]) for k in range(1, count)]


def _add(terms):
    while len(terms) > 1:
        terms = [terms[i] + terms[i + 1] for i in range(0, len(terms), 2)]
    return terms[0]


def _sum_over(x, dims):
    for dim in dims:
        x = _add(_exchange(x, *dim))
    return x


def _collect_over(x, mark, dims):
    for axis, step, count in dims:
        terms = _exchange(x, axis, step, count)
        place = lax.rem(lax.axis_index(axis) // step, count)
        parts = []
        for j in range(count):
            part = terms[0][:mark]
            for k in range(1, count):
                part = jnp.where(place ^ k == j, terms[k][:mark], part)
            parts.append(part)
        x = jnp.concatenate(parts + [_add([term[mark:] for term in terms])], axis=0)
        mark *= count
    return x


OVER_COL = (("col", 2, 4), ("col", 1, 2))
OVER_ROW = (("row", 1, 4), ("row", 4, 4))


def _sibling(x):
    return lax.ppermute(x, "col", [(i, i ^ 1) for i in range(lax.axis_size("col"))])


def _along_z(x, step):
    size = lax.axis_size("col")
    return lax.ppermute(x, "col", [(i, (i + 2 * step) % size) for i in range(size)])


def _shift_row(x, k):
    return lax.ppermute(x, "row", [(i, i ^ k) for i in range(lax.axis_size("row"))])


def _reduce_chunks(other, own, half):
    sums = {}
    crossed = {}
    for d in (2, 1, 3, 0):
        crossed[d] = _sibling(other[d])
    sums[2] = own[2].astype(F32) + crossed[2].astype(F32)
    sums[2], crossed[1], crossed[3] = lax.optimization_barrier((sums[2], crossed[1], crossed[3]))
    for d in (1, 3):
        sums[d] = own[d].astype(F32) + crossed[d].astype(F32)
    far_a = _along_z(sums[2][:half].astype(BF16), 1)
    far_b = _along_z(sums[2][half:].astype(BF16), -1)
    up_b = _along_z(sums[1][half:].astype(BF16), 1)
    down_a = _along_z(sums[3][:half].astype(BF16), -1)
    up_a = _along_z((sums[1][:half] + far_a.astype(F32)).astype(BF16), 1)
    down_b = _along_z((sums[3][half:] + far_b.astype(F32)).astype(BF16), -1)
    return own[0], crossed[0], up_a, up_b, down_a, down_b


def _gather_chunks(x, half, shares):
    a, b = x[:half], x[half:]
    up_a = _along_z(a, 1)
    down_b = _along_z(b, -1)
    up_b = _along_z(b, 1)
    down_a = _along_z(a, -1)
    first = [_sibling(x)]
    shares = [shares[0]] + [_shift_row(shares[k], k) for k in range(1, 4)]
    up_a, down_b, *shares = lax.optimization_barrier((up_a, down_b, *shares))
    far_a = _along_z(up_a, 1)
    far_b = _along_z(down_b, -1)
    first += [_sibling(up_a), _sibling(down_b)]
    up_b, down_a, *first = lax.optimization_barrier((up_b, down_a, *first))
    crossed = first + [_sibling(up_b), _sibling(down_a), _sibling(far_a), _sibling(far_b)]
    rows = [x, up_a, down_b, up_b, down_a, far_a, far_b]
    at = [(0, 0), (3, 0), (1, half), (3, half), (1, 0), (2, 0), (2, half)]
    found = [((d, False, start), part) for (d, start), part in zip(at, rows)]
    return found + [((d, True, start), part) for (d, start), part in zip(at, crossed)], shares


def _ring(x, axis):
    size = lax.axis_size(axis)
    return lax.ppermute(x, axis, [(i, (i + 1) % size) for i in range(size)])


def _ring_gather(x, axis):
    size, me, rows = lax.axis_size(axis), lax.axis_index(axis), x.shape[0]

    def step(i, carry):
        block, out = carry
        block = _ring(block, axis)
        at = lax.rem(me - i + size, size) * rows
        return block, lax.dynamic_update_slice(out, block, (at, 0))

    out = lax.dynamic_update_slice(jnp.zeros((size * rows, x.shape[1]), x.dtype), x, (me * rows, 0))
    return lax.fori_loop(1, size, step, (x, out))[1]


def _ring_reduce(x, axis):
    size, me = lax.axis_size(axis), lax.axis_index(axis)
    rows = x.shape[0] // size

    def part(i):
        return lax.dynamic_slice(x, (lax.rem(me - 1 - i + 2 * size, size) * rows, 0), (rows, x.shape[1]))

    return lax.fori_loop(1, size, lambda i, total: _ring(total, axis) + part(i), part(0))


def _general(features, cotangent, self_weight, neigh_weight, kernel, needed, src_slot, dst_local, bucket):
    row_count = lax.axis_size("row")
    col_count = lax.axis_size("col")
    node_rows = features.shape[0]
    channels = features.shape[1]
    wanted = needed.reshape(row_count, -1)
    capacity = wanted.shape[1]
    slot_ids = src_slot.reshape(-1)
    dest_ids = dst_local.reshape(-1)
    bucket_ids = bucket.reshape(-1)
    block_rows = col_count * node_rows
    one_hot = (bucket_ids[:, None] == jnp.arange(kernel.shape[0], dtype=I32)[None, :]).astype(F32)
    kernel_rows = jnp.dot(one_hot, kernel, precision=lax.Precision.HIGHEST, preferred_element_type=F32)
    gathered = _ring_gather(features, "row")
    gathered_index = slot_ids // capacity * node_rows + wanted.reshape(-1)[slot_ids]
    source_float = gathered[gathered_index].astype(F32)
    messages = kernel_rows * source_float
    summed_part = jax.ops.segment_sum(messages, dest_ids, num_segments=block_rows + 1)[:-1]
    count_part = jax.ops.segment_sum(jnp.ones(dest_ids.shape, F32), dest_ids, num_segments=block_rows + 1)[:-1]
    summed = _ring_reduce(summed_part, "col")
    degree = _ring_reduce(count_part.reshape(-1, 128), "col").reshape(-1)
    divisor = jnp.maximum(degree, 1.0)[:, None]
    mean = (summed / divisor).astype(BF16)
    preact = jnp.dot(features, self_weight, preferred_element_type=F32) + jnp.dot(
        mean, neigh_weight, preferred_element_type=F32
    )
    sigmoid_z = jax.nn.sigmoid(preact)
    out_rows = (preact * sigmoid_z).astype(BF16)
    pre_grad = (cotangent.astype(F32) * sigmoid_z * (1.0 + preact * (1.0 - sigmoid_z))).astype(BF16)
    weight_part = _dot(jnp.concatenate([features, mean], axis=1), pre_grad, TN)
    mean_grad = (_dot(pre_grad, neigh_weight, NT) / divisor).astype(BF16)
    grads = _sum_over(weight_part, OVER_COL + OVER_ROW)
    block_grad = _ring_gather(mean_grad, "col")
    padded = jnp.concatenate([block_grad, jnp.zeros((1, channels), BF16)], axis=0)
    dest_rows = padded[dest_ids].astype(F32)
    kernel_part = lax.dot_general(
        one_hot, dest_rows * source_float, TN, precision=lax.Precision.HIGHEST, preferred_element_type=F32
    )
    source_part = jax.ops.segment_sum(kernel_rows * dest_rows, gathered_index, num_segments=row_count * node_rows)
    neigh_dx = _ring_reduce(source_part, "row")
    feature_grad = _dot(pre_grad, self_weight, NT) + neigh_dx
    kernel_grad = _sum_over(kernel_part, OVER_COL + OVER_ROW)
    return (out_rows, feature_grad, grads[:128], grads[128:], kernel_grad)


def _shape(shape, dtype):
    return jax.ShapeDtypeStruct(shape, dtype)


def per_device(features, cotangent, self_weight, neigh_weight, kernel, needed, src_slot, dst_local, bucket):
    rows = lax.axis_size("row")
    cols = lax.axis_size("col")
    nodes = features.shape[0]
    edges = src_slot.shape[-1]
    line = (1, edges)
    s_line, d_line, b_line = src_slot.reshape(line), dst_local.reshape(line), bucket.reshape(line)
    req, place, num = _call(
        _ask_kernel,
        (_shape((rows, CAP), I32), _shape(line, I32), _shape((rows, 128), I32)),
        [VM] * 3,
        name="ask",
    )(s_line, d_line, needed.reshape(rows, -1))
    asked = lax.all_to_all(req, "row", 0, 0, tiled=True)
    dst, hot, same, cnt = _call(
        _slots_kernel,
        (
            _shape((rows, CAP), I32),
            _shape((rows, 16, CAP), BF16),
            _shape((rows, CAP, CAP), BF16),
            _shape((128, 128), F32),
        ),
        [VM] * 4,
        limit=24,
        name="slots",
    )(s_line, d_line, b_line, place)
    dst = dst.reshape(-1)
    served, flag = _call(
        _serve_kernel,
        (_shape((rows, CAP, 128), BF16), _shape((8, 128), F32)),
        [VM] * 2,
        name="serve",
    )(asked, features)
    source = lax.all_to_all(served, "row", 0, 0, tiled=True)
    me = lax.axis_index("col").astype(I32).reshape(1)
    half = nodes // 2
    other, own_sums = _call(
        _scatter_kernel,
        tuple([_shape((cols // 2, nodes + EXTRA, 128), BF16)] * 2),
        [SM, SM, SM, VM, VM, VM, ANY, VM, VM],
        [
            pltpu.VMEM((cols * nodes, 128), F32),
            pltpu.VMEM((rows * CAP, 128), F32),
            pltpu.VMEM(same.shape, BF16),
            pltpu.SemaphoreType.DMA,
        ],
        limit=48,
        name="scatter",
    )(me, dst, num, source, hot, kernel, same, cnt, flag)
    sums = _reduce_chunks(other, own_sums, half)
    out_rows, pre_grad, mean, mean_grad, over = _call(
        _dense_kernel,
        tuple([_shape((nodes, 128), BF16)] * 4) + (_shape((8, 128), F32),),
        [VM] * 10,
        name="dense",
    )(*sums, features, cotangent, self_weight, neigh_weight)
    share = 64
    place = lax.rem(lax.axis_index("row"), 4).astype(I32).reshape(1)
    shares = _call(
        _weights_kernel, tuple([_shape((share, 128), F32)] * 4), [SM] + [VM] * 3, name="weights"
    )(place, features, mean, pre_grad)
    found, shares = _gather_chunks(mean_grad, half, shares)
    places = [at for at, _ in found]
    sent, kernel_part = _call(
        functools.partial(_edge_grad_kernel, places),
        (_shape((rows, CAP, 128), BF16), _shape((16, 128), F32)),
        [SM, SM, SM] + [VM] * (3 + len(places)),
        [pltpu.VMEM((cols * nodes, 128), F32), pltpu.VMEM((rows * CAP, 128), F32)],
        limit=36,
        name="edge_grad",
    )(me, dst, num, source, hot, kernel, *[part for _, part in found])
    back = lax.all_to_all(sent, "row", 0, 0, tiled=True)
    grads = _call(_join_kernel, _shape((share + 16, 128), F32), [VM] * 5, flops=1 << 34, name="join")(
        *shares, kernel_part
    )
    own = _dot(pre_grad, self_weight, NT)
    grads = _sum_over(grads, OVER_COL + OVER_ROW[1:])
    back, grads = lax.optimization_barrier((back, grads))
    grads = _collect_over(grads, share, OVER_ROW[:1])
    feature_grad = _call(_collect_kernel, _shape((nodes, 128), F32), [VM] * 4, name="collect")(
        asked, asked.reshape(1, -1), back, own
    )
    outs = (out_rows, feature_grad, grads[:128], grads[128:256], grads[256:])
    inputs = (features, cotangent, self_weight, neigh_weight, kernel, needed, src_slot, dst_local, bucket)
    state = lax.while_loop(
        lambda state: state[0], lambda state: (jnp.zeros((), bool), _general(*inputs)), (over[0, 0] > 0, outs)
    )
    return state[1]


def solution(mesh):
    placed = (
        P(("row", "col"), None),
        P(("row", "col"), None),
        P(),
        P(),
        P(),
        P("row", "col", None, None),
        P("row", "col", None),
        P("row", "col", None),
        P("row", "col", None),
    )
    return jax.shard_map(
        per_device,
        mesh=mesh,
        in_specs=placed,
        out_specs=(P(("row", "col"), None), P(("row", "col"), None), P(), P(), P()),
        check_vma=False,
    )
```

```python
import functools

import jax
import jax.numpy as jnp
from jax import lax
from jax.experimental import pallas as pl
from jax.experimental.pallas import tpu as pltpu
from jax.sharding import PartitionSpec as P

BF16 = jnp.bfloat16
F32 = jnp.float32
I32 = jnp.int32

CAP = 320
BATCH = 16
FETCH = 64
GROUP = 4
ROWS = 16384
EXTRA = 64
NT = (((1,), (1,)), ((), ()))
TN = (((0,), (0,)), ((), ()))
NN = (((1,), (0,)), ((), ()))


def _dot(a, b, dims):
    return lax.dot_general(a, b, dims, preferred_element_type=F32)


def _iota(shape, dim):
    return lax.broadcasted_iota(I32, shape, dim)


def _hot(mask):
    return jnp.where(mask, 1.0, 0.0).astype(BF16)


def _ask_kernel(s_ref, d_ref, need_ref, req_ref, p_ref, num_ref):
    owners = req_ref.shape[0]
    edges = s_ref.shape[1]
    blocks = edges // 128
    need = jnp.concatenate([need_ref[:, h * 128 : (h + 1) * 128] for h in range(8)], axis=0)
    table = jnp.concatenate([(need >> 8).astype(F32), (need & 255).astype(F32)], axis=0).astype(BF16)
    owner = jnp.where(d_ref[...] < ROWS, s_ref[...] >> 10, owners)
    own = _iota((owners, edges), 0) == owner
    own_hot = _hot(own)
    stacked = jnp.concatenate([own_hot[:, b * 128 : (b + 1) * 128] for b in range(blocks)], axis=0)
    before = _hot(_iota((128, 128), 0) < _iota((128, 128), 1))
    ones = jnp.ones((128, 128), BF16)
    ranks = _dot(stacked, jnp.concatenate([before, ones], axis=1), NN)
    carry = jnp.zeros((owners, 128), F32)
    for b in range(blocks):
        part = ranks[b * owners : (b + 1) * owners]
        mine = own[:, b * 128 : (b + 1) * 128]
        p_ref[:, b * 128 : (b + 1) * 128] = jnp.sum(
            jnp.where(mine, part[:, :128] + carry, 0.0), axis=0, keepdims=True
        ).astype(I32)
        carry = carry + part[:, 128:]
    num_ref[...] = jnp.minimum(carry, float(CAP)).astype(I32)
    over = jnp.max(carry) > float(CAP)

    out = jnp.zeros((3 * owners, CAP), F32)
    step = 512
    for c in range(edges // step):
        at = slice(c * step, (c + 1) * step)
        sc = s_ref[:, at]
        low = _hot(_iota((128, step), 0) == (sc & 127))
        found = _dot(table, low, NN)
        high = _iota((128, step), 0) == ((sc >> 7) & 7) * owners + (sc >> 10)
        q_hi = jnp.sum(jnp.where(high, found[:128], 0.0), axis=0, keepdims=True)
        q_lo = jnp.sum(jnp.where(high, found[128:], 0.0), axis=0, keepdims=True)
        mine = own[:, at]
        values = [q_hi, q_lo, jnp.ones((1, step), F32)]
        spread = jnp.concatenate([jnp.where(mine, v, 0.0) for v in values], axis=0).astype(BF16)
        place = _hot(_iota((CAP, step), 0) == p_ref[:, at])
        out += _dot(spread, place, NT)
    asked = jnp.where(out[2 * owners :] > 0.5, out[:owners] * 256.0 + out[owners : 2 * owners], 2048.0)
    req_ref[...] = jnp.where(over, 4096.0, asked).astype(I32)


def _slots_kernel(s_ref, d_ref, b_ref, p_ref, dst_ref, hot_ref, same_ref, cnt_ref):
    owners = dst_ref.shape[0]
    edges = s_ref.shape[1]
    lane_out = jnp.zeros((3 * owners, CAP), F32)
    col_out = jnp.zeros((CAP, 2 * owners), F32)
    counts = jnp.zeros((128, 128), F32)
    step = 512
    for c in range(edges // step):
        at = slice(c * step, (c + 1) * step)
        dc = d_ref[:, at]
        okc = dc < ROWS
        mine = _iota((owners, step), 0) == jnp.where(okc, s_ref[:, at] >> 10, owners)
        back = jnp.maximum(ROWS - 1 - dc, 0)
        values = [(back >> 8).astype(F32), (back & 255).astype(F32), (b_ref[:, at] + 1).astype(F32)]
        spread = jnp.concatenate([jnp.where(mine, v, 0.0) for v in values], axis=0).astype(BF16)
        place = _hot(_iota((CAP, step), 0) == p_ref[:, at])
        lane_out += _dot(spread, place, NT)
        col_out += _dot(place, spread[: 2 * owners], NT)
        d_hi = _hot((_iota((128, step), 0) == (dc >> 7)) & okc)
        d_lo = _hot(_iota((128, step), 0) == (dc & 127))
        counts += _dot(d_hi, d_lo, NT)
    cnt_ref[...] = counts
    drow = lane_out[:owners] * 256.0 + lane_out[owners : 2 * owners]
    dcol = col_out[:, :owners] * 256.0 + col_out[:, owners:]
    dst_ref[...] = (float(ROWS - 1) - drow).astype(I32)
    bucket = lane_out[2 * owners :].astype(I32) - 1
    together = (_iota((CAP, CAP), 0) // BATCH) == (_iota((CAP, CAP), 1) // BATCH)
    for o in range(owners):
        hot_ref[o] = _hot(_iota((16, CAP), 0) == bucket[o : o + 1, :])
        same_ref[o] = _hot((dcol[:, o : o + 1] == drow[o : o + 1, :]) & together)


def _serve_kernel(req_ref, feat_ref, out_ref, flag_ref):
    peers = req_ref.shape[0]
    wide = jnp.concatenate([feat_ref[i * 512 : (i + 1) * 512, :] for i in range(4)], axis=1)
    req = req_ref[...]
    flag_ref[...] = jnp.broadcast_to(jnp.max(jnp.where(req >= 4096, 1.0, 0.0), keepdims=True), flag_ref.shape)
    cols = jnp.transpose(req.astype(F32)).astype(I32)
    for g in range(peers // GROUP):
        peers_of = range(g * GROUP, (g + 1) * GROUP)
        hots = [_hot(_iota((CAP, 512), 1) == (cols[:, r : r + 1] & 511)) for r in peers_of]
        got = _dot(jnp.concatenate(hots, axis=0), wide, NN)
        for k, r in enumerate(peers_of):
            part = cols[:, r : r + 1] >> 9
            mine = got[k * CAP : (k + 1) * CAP]
            rows = jnp.where(part == 0, mine[:, :128], 0.0)
            for i in range(1, 4):
                rows = jnp.where(part == i, mine[:, i * 128 : (i + 1) * 128], rows)
            out_ref[r] = rows.astype(BF16)


def _kernel_parts(kern):
    high = kern.astype(BF16)
    return jnp.concatenate([high, (kern - high.astype(F32)).astype(BF16)], axis=0)


def _kernel_rows(hot, parts):
    return _dot(jnp.concatenate([hot, hot], axis=0), parts, TN)


def _scatter_kernel(
    me_s, dst_s, num_s, rows_ref, hot_ref, kern_ref, same_hbm, cnt_ref, flag_ref, other_ref, own_ref, acc, msg, same_ref, sem
):
    owners = rows_ref.shape[0]
    copy = pltpu.make_async_copy(same_hbm, same_ref, sem)
    copy.start()
    parts = _kernel_parts(kern_ref[...])
    chunks = own_ref.shape[0]
    node_rows = own_ref.shape[1] - EXTRA

    def clear(i, c):
        acc[pl.ds(pl.multiple_of(i * 256, 256), 256), :] = jnp.zeros((256, 128), F32)
        return c

    lax.fori_loop(0, acc.shape[0] // 256, clear, 0)
    copy.wait()
    for o in range(owners):
        m = _kernel_rows(hot_ref[o], parts) * rows_ref[o].astype(F32)
        high = m.astype(BF16)
        low = (m - high.astype(F32)).astype(BF16)
        sums = _dot(same_ref[o], jnp.concatenate([high, low], axis=1), NN)
        msg[o * CAP : (o + 1) * CAP, :] = sums[:, :128] + sums[:, 128:]
    for o in range(owners):

        def batch(i, c):
            base = pl.multiple_of(o * CAP + i * BATCH, BATCH)
            at = [dst_s[base + k] for k in range(BATCH)]
            new = [acc[pl.ds(at[k], 1), :] + msg[pl.ds(base + k, 1), :] for k in range(BATCH)]
            for k in range(BATCH):
                acc[pl.ds(at[k], 1), :] = new[k]
            return c

        lax.fori_loop(0, (num_s[o, 0] + BATCH - 1) // BATCH, batch, 0)
    flag = flag_ref[0:1, :]
    z = me_s[0] // 2
    core = me_s[0] % 2
    for d in range(chunks):
        for ref, side in ((other_ref.at[d], 1 - core), (own_ref.at[d], core)):
            chunk = lax.rem(z + d, chunks) * 2 + side

            def down(i, s):
                to = pl.multiple_of(i * 256, 256)
                at = pl.multiple_of(chunk * node_rows + i * 256, 256)
                ref[pl.ds(to, 256), :] = acc[pl.ds(at, 256), :].astype(ref.dtype)
                return s

            lax.fori_loop(0, node_rows // 256, down, 0)
            cnt = cnt_ref[pl.ds(pl.multiple_of(chunk * 16, 16), 16), :].astype(I32)
            digits = [cnt & 31, (cnt >> 5) & 31, cnt >> 10]
            for j, digit in enumerate(digits):
                ref[node_rows + 16 * j : node_rows + 16 * (j + 1), :] = digit.astype(F32).astype(ref.dtype)
            ref[node_rows + 48 : node_rows + 64, :] = jnp.broadcast_to(flag, (16, 128)).astype(ref.dtype)


def _dense_kernel(own_ref, core_ref, up_a_ref, up_b_ref, down_a_ref, down_b_ref, feat_ref, cot_ref, ws_ref, wn_ref, out_ref, pg_ref, mean_ref, mg_ref, flag_ref):
    node_rows = feat_ref.shape[0]
    half = up_a_ref.shape[0]

    def summed(start, size):
        total = own_ref[start : start + size, :].astype(F32) + core_ref[start : start + size, :].astype(F32)
        first, second, at = (up_a_ref, down_a_ref, start) if start < half else (up_b_ref, down_b_ref, start - half)
        return total + first[at : at + size, :].astype(F32) + second[at : at + size, :].astype(F32)

    digit = [summed(node_rows + 16 * j, 16) for j in range(3)]
    flag_ref[...] = summed(node_rows + 48, 8)
    degree = digit[0] + 32.0 * digit[1] + 1024.0 * digit[2]
    div_cols = jnp.transpose(jnp.maximum(degree, 1.0))
    both = jnp.concatenate([ws_ref[...], wn_ref[...]], axis=0)
    wn = wn_ref[...]
    for i in range(node_rows // 128):
        at = slice(i * 128, (i + 1) * 128)
        div = div_cols[:, i : i + 1]
        mean = (summed(i * 128, 128) / div).astype(BF16)
        z = _dot(jnp.concatenate([feat_ref[at, :], mean], axis=1), both, NN)
        sig = jax.nn.sigmoid(z)
        pg = (cot_ref[at, :].astype(F32) * sig * (1.0 + z * (1.0 - sig))).astype(BF16)
        out_ref[at, :] = (z * sig).astype(BF16)
        pg_ref[at, :] = pg
        mean_ref[at, :] = mean
        mg_ref[at, :] = (_dot(pg, wn, NT) / div).astype(BF16)


def _weights_kernel(place_s, feat_ref, mean_ref, pg_ref, *share_refs):
    pg = pg_ref[...]
    parts = [_dot(feat_ref[...], pg, TN), _dot(mean_ref[...], pg, TN)]
    rows = share_refs[0].shape[0]
    quarters = [part[i * rows : (i + 1) * rows] for part in parts for i in range(2)]
    for k, ref in enumerate(share_refs):
        which = place_s[0] ^ k
        share = quarters[0]
        for j in range(1, 4):
            share = jnp.where(which == j, quarters[j], share)
        ref[...] = share


def _edge_grad_kernel(places, me_s, dst_s, num_s, rows_ref, hot_ref, kern_ref, *refs):
    owners = rows_ref.shape[0]
    out_ref, sum_ref, table, got = refs[len(places) :]
    z = me_s[0] // 2
    core = me_s[0] % 2
    zs = table.shape[0] // 4096
    for ref, (d, other, start) in zip(refs, places):
        chunk = lax.rem(z + d, zs) * 2 + (1 - core if other else core)

        def widen(i, c):
            at = pl.multiple_of(chunk * 2048 + start + i * 256, 256)
            table[pl.ds(at, 256), :] = ref[pl.ds(pl.multiple_of(i * 256, 256), 256), :].astype(F32)
            return c

        lax.fori_loop(0, ref.shape[0] // 256, widen, 0)
    got[...] = jnp.zeros(got.shape, F32)
    for o in range(owners):

        def batch(i, c):
            base = pl.multiple_of(o * CAP + i * FETCH, FETCH)
            at = [dst_s[base + k] for k in range(FETCH)]
            for k in range(FETCH):
                got[pl.ds(base + k, 1), :] = table[pl.ds(at[k], 1), :]
            return c

        lax.fori_loop(0, (num_s[o, 0] + FETCH - 1) // FETCH, batch, 0)
    parts = _kernel_parts(kern_ref[...])
    total = jnp.zeros((16, 128), F32)
    for o in range(owners):
        g = got[o * CAP : (o + 1) * CAP, :]
        out_ref[o] = (_kernel_rows(hot_ref[o], parts) * g).astype(BF16)
        total += _dot(hot_ref[o], (g * rows_ref[o].astype(F32)).astype(BF16), NN)
    sum_ref[...] = total


def _join_kernel(*refs):
    shares, kern_ref, out_ref = refs[:-2], refs[-2], refs[-1]
    rows = shares[0].shape[0]
    out_ref[:rows, :] = _add([share[...] for share in shares])
    out_ref[rows:, :] = kern_ref[...]


def _collect_kernel(req_ref, line_ref, part_ref, dense_ref, out_ref):
    peers = req_ref.shape[0]
    cols = jnp.transpose(req_ref[...].astype(F32)).astype(I32) >> 9
    total = jnp.concatenate([dense_ref[i * 512 : (i + 1) * 512, :] for i in range(4)], axis=1)
    wide = GROUP * CAP
    for g in range(peers // GROUP):
        hots = _hot(_iota((512, wide), 0) == (line_ref[:, g * wide : (g + 1) * wide] & 511))
        spread = []
        for r in range(g * GROUP, (g + 1) * GROUP):
            rows = part_ref[r].astype(F32)
            block = cols[:, r : r + 1]
            spread.append(jnp.concatenate([jnp.where(block == i, rows, 0.0).astype(BF16) for i in range(4)], axis=1))
        total = total + _dot(hots, jnp.concatenate(spread, axis=0), NN)
    for i in range(4):
        out_ref[i * 512 : (i + 1) * 512, :] = total[:, i * 128 : (i + 1) * 128]


VM = pl.BlockSpec(memory_space=pltpu.VMEM)
SM = pl.BlockSpec(memory_space=pltpu.SMEM)
ANY = pl.BlockSpec(memory_space=pl.ANY)


def _call(kernel, out_shape, in_specs, scratch=(), limit=16, flops=1 << 31, name=None):
    return pl.pallas_call(
        kernel,
        out_shape=out_shape,
        in_specs=in_specs,
        out_specs=jax.tree.map(lambda _: VM, out_shape),
        scratch_shapes=list(scratch),
        compiler_params=pltpu.CompilerParams(vmem_limit_bytes=limit << 20),
        cost_estimate=pl.CostEstimate(flops=flops, bytes_accessed=4 << 20, transcendentals=0),
        name=name,
    )


def _exchange(x, axis, step, count):
    size = lax.axis_size(axis)
    return [x] + [lax.ppermute(x, axis, [(i, i ^ (k * step)) for i in range(size)]) for k in range(1, count)]


def _add(terms):
    while len(terms) > 1:
        terms = [terms[i] + terms[i + 1] for i in range(0, len(terms), 2)]
    return terms[0]


def _sum_over(x, dims):
    for dim in dims:
        x = _add(_exchange(x, *dim))
    return x


def _collect_over(x, mark, axis, step, count):
    terms = _exchange(x, axis, step, count)
    place = lax.rem(lax.axis_index(axis) // step, count)
    parts = []
    for j in range(count):
        part = terms[0][:mark]
        for k in range(1, count):
            part = jnp.where(place ^ k == j, terms[k][:mark], part)
        parts.append(part)
    return parts, _add([term[mark:] for term in terms])


OVER_COL = (("col", 2, 4), ("col", 1, 2))
OVER_ROW = (("row", 1, 4), ("row", 4, 4))


def _sibling(x):
    return lax.ppermute(x, "col", [(i, i ^ 1) for i in range(lax.axis_size("col"))])


def _along_z(x, step):
    size = lax.axis_size("col")
    return lax.ppermute(x, "col", [(i, (i + 2 * step) % size) for i in range(size)])


def _shift_row(x, k):
    return lax.ppermute(x, "row", [(i, i ^ k) for i in range(lax.axis_size("row"))])


def _reduce_chunks(other, own, half):
    sums = {}
    crossed = {}
    for d in (2, 1, 3, 0):
        crossed[d] = _sibling(other[d])
    sums[2] = own[2].astype(F32) + crossed[2].astype(F32)
    sums[2], crossed[1], crossed[3] = lax.optimization_barrier((sums[2], crossed[1], crossed[3]))
    for d in (1, 3):
        sums[d] = own[d].astype(F32) + crossed[d].astype(F32)
    far_a = _along_z(sums[2][:half].astype(BF16), 1)
    far_b = _along_z(sums[2][half:].astype(BF16), -1)
    up_b = _along_z(sums[1][half:].astype(BF16), 1)
    down_a = _along_z(sums[3][:half].astype(BF16), -1)
    up_a = _along_z((sums[1][:half] + far_a.astype(F32)).astype(BF16), 1)
    down_b = _along_z((sums[3][half:] + far_b.astype(F32)).astype(BF16), -1)
    return own[0], crossed[0], up_a, up_b, down_a, down_b


def _gather_chunks(x, half, shares):
    a, b = x[:half], x[half:]
    up_a = _along_z(a, 1)
    down_b = _along_z(b, -1)
    up_b = _along_z(b, 1)
    down_a = _along_z(a, -1)
    first = [_sibling(x)]
    shares = [shares[0]] + [_shift_row(shares[k], k) for k in range(1, 4)]
    up_a, down_b, *shares = lax.optimization_barrier((up_a, down_b, *shares))
    far_a = _along_z(up_a, 1)
    far_b = _along_z(down_b, -1)
    first += [_sibling(up_a), _sibling(down_b)]
    up_b, down_a, *first = lax.optimization_barrier((up_b, down_a, *first))
    crossed = first + [_sibling(up_b), _sibling(down_a), _sibling(far_a), _sibling(far_b)]
    rows = [x, up_a, down_b, up_b, down_a, far_a, far_b]
    at = [(0, 0), (3, 0), (1, half), (3, half), (1, 0), (2, 0), (2, half)]
    found = [((d, False, start), part) for (d, start), part in zip(at, rows)]
    return found + [((d, True, start), part) for (d, start), part in zip(at, crossed)], shares


def _ring(x, axis):
    size = lax.axis_size(axis)
    return lax.ppermute(x, axis, [(i, (i + 1) % size) for i in range(size)])


def _ring_gather(x, axis):
    size, me, rows = lax.axis_size(axis), lax.axis_index(axis), x.shape[0]

    def step(i, carry):
        block, out = carry
        block = _ring(block, axis)
        at = lax.rem(me - i + size, size) * rows
        return block, lax.dynamic_update_slice(out, block, (at, 0))

    out = lax.dynamic_update_slice(jnp.zeros((size * rows, x.shape[1]), x.dtype), x, (me * rows, 0))
    return lax.fori_loop(1, size, step, (x, out))[1]


def _ring_reduce(x, axis):
    size, me = lax.axis_size(axis), lax.axis_index(axis)
    rows = x.shape[0] // size

    def part(i):
        return lax.dynamic_slice(x, (lax.rem(me - 1 - i + 2 * size, size) * rows, 0), (rows, x.shape[1]))

    return lax.fori_loop(1, size, lambda i, total: _ring(total, axis) + part(i), part(0))


def _general(features, cotangent, self_weight, neigh_weight, kernel, needed, src_slot, dst_local, bucket):
    row_count = lax.axis_size("row")
    col_count = lax.axis_size("col")
    node_rows = features.shape[0]
    channels = features.shape[1]
    wanted = needed.reshape(row_count, -1)
    capacity = wanted.shape[1]
    slot_ids = src_slot.reshape(-1)
    dest_ids = dst_local.reshape(-1)
    bucket_ids = bucket.reshape(-1)
    block_rows = col_count * node_rows
    one_hot = (bucket_ids[:, None] == jnp.arange(kernel.shape[0], dtype=I32)[None, :]).astype(F32)
    kernel_rows = jnp.dot(one_hot, kernel, precision=lax.Precision.HIGHEST, preferred_element_type=F32)
    gathered = _ring_gather(features, "row")
    gathered_index = slot_ids // capacity * node_rows + wanted.reshape(-1)[slot_ids]
    source_float = gathered[gathered_index].astype(F32)
    messages = kernel_rows * source_float
    summed_part = jax.ops.segment_sum(messages, dest_ids, num_segments=block_rows + 1)[:-1]
    count_part = jax.ops.segment_sum(jnp.ones(dest_ids.shape, F32), dest_ids, num_segments=block_rows + 1)[:-1]
    summed = _ring_reduce(summed_part, "col")
    degree = _ring_reduce(count_part.reshape(-1, 128), "col").reshape(-1)
    divisor = jnp.maximum(degree, 1.0)[:, None]
    mean = (summed / divisor).astype(BF16)
    preact = jnp.dot(features, self_weight, preferred_element_type=F32) + jnp.dot(
        mean, neigh_weight, preferred_element_type=F32
    )
    sigmoid_z = jax.nn.sigmoid(preact)
    out_rows = (preact * sigmoid_z).astype(BF16)
    pre_grad = (cotangent.astype(F32) * sigmoid_z * (1.0 + preact * (1.0 - sigmoid_z))).astype(BF16)
    weight_part = _dot(jnp.concatenate([features, mean], axis=1), pre_grad, TN)
    mean_grad = (_dot(pre_grad, neigh_weight, NT) / divisor).astype(BF16)
    grads = _sum_over(weight_part, OVER_COL + OVER_ROW)
    block_grad = _ring_gather(mean_grad, "col")
    padded = jnp.concatenate([block_grad, jnp.zeros((1, channels), BF16)], axis=0)
    dest_rows = padded[dest_ids].astype(F32)
    kernel_part = lax.dot_general(
        one_hot, dest_rows * source_float, TN, precision=lax.Precision.HIGHEST, preferred_element_type=F32
    )
    source_part = jax.ops.segment_sum(kernel_rows * dest_rows, gathered_index, num_segments=row_count * node_rows)
    neigh_dx = _ring_reduce(source_part, "row")
    feature_grad = _dot(pre_grad, self_weight, NT) + neigh_dx
    kernel_grad = _sum_over(kernel_part, OVER_COL + OVER_ROW)
    return (out_rows, feature_grad, grads[:128], grads[128:], kernel_grad)


def _shape(shape, dtype):
    return jax.ShapeDtypeStruct(shape, dtype)


def per_device(features, cotangent, self_weight, neigh_weight, kernel, needed, src_slot, dst_local, bucket):
    rows = lax.axis_size("row")
    cols = lax.axis_size("col")
    nodes = features.shape[0]
    edges = src_slot.shape[-1]
    line = (1, edges)
    s_line, d_line, b_line = src_slot.reshape(line), dst_local.reshape(line), bucket.reshape(line)
    req, place, num = _call(
        _ask_kernel,
        (_shape((rows, CAP), I32), _shape(line, I32), _shape((rows, 128), I32)),
        [VM] * 3,
        name="ask",
    )(s_line, d_line, needed.reshape(rows, -1))
    asked = lax.all_to_all(req, "row", 0, 0, tiled=True)
    dst, hot, same, cnt = _call(
        _slots_kernel,
        (
            _shape((rows, CAP), I32),
            _shape((rows, 16, CAP), BF16),
            _shape((rows, CAP, CAP), BF16),
            _shape((128, 128), F32),
        ),
        [VM] * 4,
        limit=24,
        name="slots",
    )(s_line, d_line, b_line, place)
    dst = dst.reshape(-1)
    served, flag = _call(
        _serve_kernel,
        (_shape((rows, CAP, 128), BF16), _shape((8, 128), F32)),
        [VM] * 2,
        name="serve",
    )(asked, features)
    source = lax.all_to_all(served, "row", 0, 0, tiled=True)
    me = lax.axis_index("col").astype(I32).reshape(1)
    half = nodes // 2
    other, own_sums = _call(
        _scatter_kernel,
        tuple([_shape((cols // 2, nodes + EXTRA, 128), BF16)] * 2),
        [SM, SM, SM, VM, VM, VM, ANY, VM, VM],
        [
            pltpu.VMEM((cols * nodes, 128), F32),
            pltpu.VMEM((rows * CAP, 128), F32),
            pltpu.VMEM(same.shape, BF16),
            pltpu.SemaphoreType.DMA,
        ],
        limit=48,
        name="scatter",
    )(me, dst, num, source, hot, kernel, same, cnt, flag)
    sums = _reduce_chunks(other, own_sums, half)
    out_rows, pre_grad, mean, mean_grad, over = _call(
        _dense_kernel,
        tuple([_shape((nodes, 128), BF16)] * 4) + (_shape((8, 128), F32),),
        [VM] * 10,
        name="dense",
    )(*sums, features, cotangent, self_weight, neigh_weight)
    share = 64
    place = lax.rem(lax.axis_index("row"), 4).astype(I32).reshape(1)
    shares = _call(
        _weights_kernel, tuple([_shape((share, 128), F32)] * 4), [SM] + [VM] * 3, name="weights"
    )(place, features, mean, pre_grad)
    found, shares = _gather_chunks(mean_grad, half, shares)
    places = [at for at, _ in found]
    sent, kernel_part = _call(
        functools.partial(_edge_grad_kernel, places),
        (_shape((rows, CAP, 128), BF16), _shape((16, 128), F32)),
        [SM, SM, SM] + [VM] * (3 + len(places)),
        [pltpu.VMEM((cols * nodes, 128), F32), pltpu.VMEM((rows * CAP, 128), F32)],
        limit=36,
        name="edge_grad",
    )(me, dst, num, source, hot, kernel, *[part for _, part in found])
    back = lax.all_to_all(sent, "row", 0, 0, tiled=True)
    grads = _call(_join_kernel, _shape((share + 16, 128), F32), [VM] * 5, flops=1 << 34, name="join")(
        *shares, kernel_part
    )
    own = _dot(pre_grad, self_weight, NT)
    grads = _sum_over(grads, OVER_COL + OVER_ROW[1:])
    back, grads = lax.optimization_barrier((back, grads))
    parts, kernel_grad = _collect_over(grads, share, *OVER_ROW[0])
    feature_grad = _call(_collect_kernel, _shape((nodes, 128), F32), [VM] * 4, name="collect")(
        asked, asked.reshape(1, -1), back, own
    )
    outs = (out_rows, feature_grad, jnp.concatenate(parts[:2]), jnp.concatenate(parts[2:]), kernel_grad)
    inputs = (features, cotangent, self_weight, neigh_weight, kernel, needed, src_slot, dst_local, bucket)
    state = lax.while_loop(
        lambda state: state[0], lambda state: (jnp.zeros((), bool), _general(*inputs)), (over[0, 0] > 0, outs)
    )
    return state[1]


def solution(mesh):
    placed = (
        P(("row", "col"), None),
        P(("row", "col"), None),
        P(),
        P(),
        P(),
        P("row", "col", None, None),
        P("row", "col", None),
        P("row", "col", None),
        P("row", "col", None),
    )
    return jax.shard_map(
        per_device,
        mesh=mesh,
        in_specs=placed,
        out_specs=(P(("row", "col"), None), P(("row", "col"), None), P(), P(), P()),
        check_vma=False,
    )
```
